32 devices in a mesh: depth: 32 (over z, y, x, core), xs: 1.
Axes of the slice: x: 2, y: 2, z: 4, core: 2. Of those that a mesh axis runs over, the one named last changes fastest.
Arguments:
- density: bfloat16 [512, 128, 512], P('depth', None, 'xs'), may hold values from 0.049804688 to 2
- clip_flags: int32 [512, 8, 4], P('depth', None, 'xs'), may hold values 0 or 1
- band_offset: int32 [1], replicated, may hold values from 0 to 3071
- order: int32 [32], replicated, may hold values from 0 to 31, as said below
- ambient: float32 [3], replicated, may hold values from 0.1 to 0.6
- diffuse: float32 [3], replicated, may hold values from 1 to 3
Outputs:
- image: float32 [4, 128, 512], P(None, 'depth', 'xs')
The draws below stay inside these ranges and needn't reach their ends.
Inputs may be any that keep to these rules, and one draw needn't show every extreme that they name: The front-to-back order of a binary space partition of the slabs: order[k] = k XOR m for one m of 0 to 31.
All inputs are finite; a program needn't handle non-finite values. No bound on the sum of `clip_flags` on one device may be relied on, other than what follows from the above.
Results may differ from the reference program's by a relative error of at most 0.0003.
Values sent between devices are 32-bit elements; how exact they have to be, the bound alone decides.
No kernel may reach another device: no remote copies, remote signals or barrier semaphores. Data moves between devices by JAX's collectives and lax.ppermute only.
A program may use at most 64 MiB of HBM per device.

```python
import math
import jax
import jax.numpy as jnp
from jax import lax

SZ = 16
ROWS = 128
RB = 16
XB = 128
NZ = 512
NX = 512
N_DEPTH = 32


def draw_order(key, part):
    mask_value = jax.random.randint(jax.random.fold_in(key, 11), (), 0, N_DEPTH, dtype=jnp.int32)
    return jnp.bitwise_xor(jnp.arange(N_DEPTH, dtype=jnp.int32), mask_value)


def set_ends(drawn, rng, low, largest):
    shape = drawn.shape
    spot = [jax.random.randint(jax.random.fold_in(rng, axis), (), 0, shape[axis]) for axis in range(len(shape))]
    drawn = drawn.at[tuple(spot)].set(low)
    longest = shape.index(max(shape))
    spot[longest] = (spot[longest] + 1) % shape[longest]
    return drawn.at[tuple(spot)].set(largest)


def block_scale(own_key, shape, split, low, top_value):
    gain, own = 1.0, jax.random.fold_in(own_key, 6)
    for axis_at, blocks in split:
        steps = jnp.exp(jax.random.uniform(jax.random.fold_in(own, axis_at), (blocks,), jnp.float32, low / len(split), top_value / len(split)))
        gain = gain * jnp.repeat(steps, shape[axis_at] // blocks).reshape([-1 if axis == axis_at else 1 for axis in range(len(shape))])
    return gain


def setup_inputs(seed: int = 0) -> dict:
    arg_keys = jax.random.split(jax.random.key(seed), 7)
    return {
        "density": jnp.clip(jnp.exp(math.log(2.0) - 3.6927934 * jax.random.uniform(arg_keys[0], (NZ, ROWS, NX), jnp.float32) ** block_scale(arg_keys[0], (NZ, ROWS, NX), ((0, 32),), -0.2, 0.2)), 0.049804688, 2.0).astype(jnp.bfloat16),
        "clip_flags": set_ends((jax.random.randint(arg_keys[1], (NZ, ROWS // RB, NX // XB), 0, 4) < 3).astype(jnp.int32), jax.random.fold_in(arg_keys[1], 1), 0, 1),
        "band_offset": jax.random.randint(arg_keys[2], (1,), 0, 3072).astype(jnp.int32),
        "order": draw_order(jax.random.fold_in(arg_keys[6], 71), 0),
        "ambient": jnp.clip(jax.random.uniform(arg_keys[4], (3,), jnp.float32, 0.1, 0.6), 0.1, 0.6),
        "diffuse": jnp.clip(jax.random.uniform(arg_keys[5], (3,), jnp.float32, 1.0, 3.0), 1.0, 3.0),
    }


def expand_flags(flags):
    slices, blocks_r, blocks_x = flags.shape
    full = jnp.broadcast_to(flags[:, :, None, :, None], (slices, blocks_r, RB, blocks_x, XB))
    return full.reshape(slices, blocks_r * RB, blocks_x * XB).astype(jnp.float32)


def slab_terms(dens_slab, flag_slab, offset, ambient, diffuse):
    kappa = 2.0 / NZ
    clipped = dens_slab.astype(jnp.float32) * expand_flags(flag_slab)
    light_depth = (2.0 / NX) * (jnp.cumsum(clipped, axis=2) - clipped)
    rows = (offset + jnp.arange(ROWS, dtype=jnp.int32)).astype(jnp.float32)
    source = 0.6 + 0.4 * jnp.cos(2.0 * math.pi * rows / 64.0)
    light = source[None, :, None] * jnp.exp(-light_depth)
    before = jnp.cumsum(clipped, axis=0) - clipped
    weight = -jnp.expm1(-kappa * clipped) * jnp.exp(-kappa * before)
    base = jnp.sum(clipped * weight, axis=0)
    lit = jnp.sum(clipped * light * weight, axis=0)
    rgb = ambient[:, None, None] * base[None] + diffuse[:, None, None] * lit[None]
    return rgb, jnp.sum(clipped, axis=0)


def reference(density, clip_flags, band_offset, order, ambient, diffuse):
    kappa = 2.0 / NZ
    offset = band_offset[0]

    def step(carry, k):
        rgb_acc, dsum = carry
        start = (order[k] * SZ).astype(jnp.int32)
        slab = lax.dynamic_slice_in_dim(density, start, SZ, 0)
        flag_slab = lax.dynamic_slice_in_dim(clip_flags, start, SZ, 0)
        rgb, total = slab_terms(slab, flag_slab, offset, ambient, diffuse)
        rgb_acc = rgb_acc + rgb * jnp.exp(-kappa * dsum)[None]
        return (rgb_acc, dsum + total), None

    init = (jnp.zeros((3, ROWS, NX), jnp.float32), jnp.zeros((ROWS, NX), jnp.float32))
    (rgb_acc, dsum), unused = lax.scan(step, init, jnp.arange(N_DEPTH, dtype=jnp.int32))
    alpha = -jnp.expm1(-kappa * dsum)
    return jnp.concatenate([rgb_acc, alpha[None]], axis=0)
```

```python
import functools
import math

import jax
import jax.numpy as jnp
from jax import lax
from jax.experimental import pallas as pl
from jax.experimental.pallas import tpu as pltpu
from jax.sharding import PartitionSpec as P

LANES = 128


def prefix(value, axis, join, neutral):
    count, mine = (lax.axis_size(axis), lax.axis_index(axis))
    pieces = lax.all_gather(value, axis)
    so_far = jnp.full_like(value, 0) + jnp.asarray(neutral, value.dtype)

    def lap(position, so_far):
        longer = join(so_far, pieces[position])
        return jnp.where(position < mine, longer, so_far)

    return lax.fori_loop(0, count - 1, lap, so_far)


def slab_kernel(depth_scale, light_scale, share_rows, has_nearer, bit_ref, flags_ref, dens_ref, *rest):
    if has_nearer:
        nearer_ref, keep_ref, give_ref, dens, masked, upper, sems = rest
    else:
        keep_ref, give_ref, dens, masked, upper, sems = rest
    slices, rows, cells = dens.shape
    blocks_r, blocks_x = flags_ref.shape[1:]
    band = rows // blocks_r
    width = cells // blocks_x
    shares = band // share_rows

    def copy(block):
        at = pl.ds(pl.multiple_of(block * band, band), band)
        return pltpu.make_async_copy(dens_ref.at[:, at, :], dens.at[:, at, :], sems.at[block])

    for block in range(blocks_r):
        copy(block).start()
    upper[...] = (
        lax.broadcasted_iota(jnp.int32, (cells, cells), 0)
        < lax.broadcasted_iota(jnp.int32, (cells, cells), 1)
    ).astype(jnp.float32).astype(jnp.bfloat16)
    odd = bit_ref[0] == 1

    def step(block, carry):
        copy(block).wait()
        at = pl.ds(pl.multiple_of(block * band, band), band)
        for z in range(slices):
            for j in range(blocks_x):
                cols = pl.ds(j * width, width)
                flag = flags_ref[z, block, j].astype(jnp.float32)
                flag = jnp.full((band, width), flag, jnp.float32).astype(jnp.bfloat16)
                masked[z, :, cols] = dens[z, at, cols] * flag
        lhs = masked[...].reshape(slices * band, cells)
        inside = jnp.dot(lhs, upper[...], preferred_element_type=jnp.float32)
        inside = inside.reshape(slices, band, cells)
        before = jnp.zeros((band, cells), jnp.float32)
        through = jnp.ones((band, cells), jnp.float32)
        base = jnp.zeros((band, cells), jnp.float32)
        lit = jnp.zeros((band, cells), jnp.float32)
        for z in range(slices):
            clipped = masked[z].astype(jnp.float32)
            before = before + clipped
            behind = jnp.exp2(before * depth_scale)
            emitted = clipped * (through - behind)
            through = behind
            shade = inside[z]
            if has_nearer:
                shade = shade + nearer_ref[z, at, :]
            base = base + emitted
            lit = lit + emitted * jnp.exp2(shade * light_scale)
        for channel, value in enumerate((base, lit, before)):
            for pair in range(shares // 2):
                halves = []
                for side in range(2):
                    first = (2 * pair + side) * share_rows
                    halves.append(
                        jnp.concatenate(
                            [
                                value[first : first + share_rows, j * LANES : (j + 1) * LANES]
                                for j in range(cells // LANES)
                            ],
                            axis=0,
                        )
                    )
                to = block * (shares // 2) + pair
                keep_ref[channel, to] = jnp.where(odd, halves[1], halves[0])
                give_ref[channel, to] = jnp.where(odd, halves[0], halves[1])
        return carry

    lax.fori_loop(0, blocks_r, step, 0)


def composite_slab(bit, clip_flags, density, nearer, kappa, extinct, depth_n):
    slices, rows, cells = density.shape
    share_rows = rows // depth_n
    half = (3, depth_n // 2, share_rows * cells // LANES, LANES)
    log2e = math.log2(math.e)
    has_nearer = nearer is not None
    smem = pl.BlockSpec(memory_space=pltpu.SMEM)
    vmem = pl.BlockSpec(memory_space=pltpu.VMEM)
    return pl.pallas_call(
        functools.partial(slab_kernel, -kappa * log2e, -extinct * log2e, share_rows, has_nearer),
        out_shape=[jax.ShapeDtypeStruct(half, jnp.float32)] * 2,
        in_specs=[smem, smem, pl.BlockSpec(memory_space=pltpu.HBM)] + [vmem] * has_nearer,
        out_specs=[vmem, vmem],
        scratch_shapes=[
            pltpu.VMEM((slices, rows, cells), jnp.bfloat16),
            pltpu.VMEM((slices, rows // clip_flags.shape[1], cells), jnp.bfloat16),
            pltpu.VMEM((cells, cells), jnp.bfloat16),
            pltpu.SemaphoreType.DMA((clip_flags.shape[1],)),
        ],
        compiler_params=pltpu.CompilerParams(vmem_limit_bytes=32 * 2**20),
        cost_estimate=pl.CostEstimate(
            flops=2 * slices * rows * cells * cells,
            bytes_accessed=2 * slices * rows * cells,
            transcendentals=2 * slices * rows * cells,
        ),
        name="slab",
    )(bit, clip_flags, density, *([nearer] if has_nearer else []))


def on_device(density, clip_flags, band_offset, order, ambient, diffuse):
    slices, rows, cells = density.shape
    depth_n = lax.axis_size("depth")
    xs_n = lax.axis_size("xs")
    kappa = 2.0 / (slices * depth_n)
    extinct = 2.0 / (cells * xs_n)
    share_rows = rows // depth_n
    levels = depth_n.bit_length() - 1
    my_slab = lax.axis_index("depth")
    my_rank = my_slab ^ order[0]
    nearer = None
    if xs_n > 1:
        blocks_r, blocks_x = clip_flags.shape[1:]
        kept = density.astype(jnp.float32).reshape(
            slices, blocks_r, rows // blocks_r, blocks_x, cells // blocks_x
        )
        totals = jnp.sum(kept, axis=4) * clip_flags[:, :, None, :].astype(jnp.float32)
        totals = jnp.sum(totals, axis=3).reshape(slices, rows)
        nearer = prefix(totals, "xs", lambda early, late: early + late, jnp.zeros_like(totals))
        nearer = nearer[:, :, None]
    bit = (my_slab & 1).astype(jnp.int32).reshape(1)
    keep, give = composite_slab(bit, clip_flags, density, nearer, kappa, extinct, depth_n)
    for level in range(levels):
        mask = 2**level
        pairs = [(source, source ^ mask) for source in range(depth_n)]
        recv = lax.ppermute(give, "depth", pairs)
        partner_front = (my_rank >> level & 1).astype(jnp.float32)
        keep_fade = jnp.exp(-kappa * partner_front * recv[2])
        recv_fade = jnp.exp(-kappa * (1.0 - partner_front) * keep[2])
        colors = keep[:2] * keep_fade[None] + recv[:2] * recv_fade[None]
        column = keep[2:] + recv[2:]
        share = jnp.concatenate([colors, column], axis=0)
        if level + 1 < levels:
            side = my_slab >> (level + 1) & 1
            split = share.reshape(3, share.shape[1] // 2, 2, *share.shape[2:])
            keep = lax.dynamic_index_in_dim(split, side, axis=2, keepdims=False)
            give = lax.dynamic_index_in_dim(split, 1 - side, axis=2, keepdims=False)
    share = share.reshape(3, cells // LANES, share_rows, LANES)
    share = share.transpose(0, 2, 1, 3).reshape(3, share_rows, cells)
    row_pos = band_offset[0] + my_slab * share_rows + jnp.arange(share_rows, dtype=jnp.int32)
    source = 0.6 + 0.4 * jnp.cos(2.0 * math.pi * row_pos.astype(jnp.float32) / 64.0)
    lit = source[:, None] * share[1]
    colors = ambient[:, None, None] * share[0][None] + diffuse[:, None, None] * lit[None]
    alpha = -jnp.expm1(-kappa * share[2])
    return jnp.concatenate([colors, alpha[None]], axis=0)


def solution(mesh):
    return jax.shard_map(
        on_device,
        mesh=mesh,
        in_specs=(P("depth", None, "xs"), P("depth", None, "xs"), P(), P(), P(), P()),
        out_specs=P(None, "depth", "xs"),
        check_vma=False,
    )
```

```python
import functools
import math

import jax
import jax.numpy as jnp
from jax import lax
from jax.experimental import pallas as pl
from jax.experimental.pallas import tpu as pltpu

from jax.sharding import PartitionSpec as P

LANES = 128

def prefix(value, axis, join, neutral):
    count, mine = (lax.axis_size(axis), lax.axis_index(axis))
    pieces = lax.all_gather(value, axis)
    so_far = jnp.full_like(value, 0) + jnp.asarray(neutral, value.dtype)

    def lap(position, so_far):
        longer = join(so_far, pieces[position])
        return jnp.where(position < mine, longer, so_far)

    return lax.fori_loop(0, count - 1, lap, so_far)


def slab_kernel(depth_scale, light_scale, share_rows, has_nearer, flags_hbm, dens_ref, *rest):
    if has_nearer:
        nearer_ref, *rest = rest
    keep_ref, give_ref, dens, masked, inside, upper, flags, sems, flag_sem = rest
    slices, rows, cells = dens.shape
    blocks_r, blocks_x = flags.shape[:2]
    band = rows // blocks_r
    width = cells // blocks_x
    span = upper.shape[0]
    group = masked.shape[2] // band
    tall = group * band
    shares = band // share_rows

    def copy(step):
        at = pl.ds(pl.multiple_of(step * tall, tall), tall)
        return pltpu.make_async_copy(dens_ref.at[:, at, :], dens.at[:, at, :], sems.at[step])

    flag_copy = pltpu.make_async_copy(flags_hbm, flags, flag_sem)
    flag_copy.start()
    for step in range(rows // tall):
        copy(step).start()
    upper[...] = (
        lax.broadcasted_iota(jnp.int32, (span, span), 0) < lax.broadcasted_iota(jnp.int32, (span, span), 1)
    ).astype(jnp.float32).astype(jnp.bfloat16)
    odd = lax.axis_index("depth") & 1 == 1
    flag_copy.wait()

    def work(step, carry):
        copy(step).wait()
        for g in range(group):
            block = step * group + g
            at = pl.ds(pl.multiple_of(block * band, band), band)
            for j in range(blocks_x):
                for z in range(slices):
                    flag = flags[block, j, z].astype(jnp.float32)
                    flag = jnp.full((band, width), flag, jnp.float32).astype(jnp.bfloat16)
                    masked[j * width // span, z, g * band : (g + 1) * band, j * width % span : j * width % span + width] = (
                        dens[z, at, j * width : (j + 1) * width] * flag
                    )
        lhs = masked[...].reshape(cells // span * slices * tall, span)
        inside[...] = jnp.dot(lhs, upper[...], preferred_element_type=jnp.float32).reshape(inside.shape)
        for g in range(group):
            sub = slice(g * band, (g + 1) * band)
            at = pl.ds(pl.multiple_of((step * group + g) * band, band), band)
            outs = []
            for j in range(cells // LANES):
                h, first = j * LANES // span, j * LANES % span
                cols = slice(first, first + LANES)
                before = jnp.zeros((band, LANES), jnp.float32)
                through = jnp.ones((band, LANES), jnp.float32)
                base = jnp.zeros((band, LANES), jnp.float32)
                lit = jnp.zeros((band, LANES), jnp.float32)
                for z in range(slices):
                    clipped = masked[h, z, sub, cols].astype(jnp.float32)
                    before = before + clipped
                    behind = jnp.exp2(before * depth_scale)
                    emitted = clipped * (through - behind)
                    through = behind
                    shade = inside[h, z, sub, cols]
                    for left in range(h):
                        shade = shade + inside[left, z, sub, span - 1 : span] + masked[left, z, sub, span - 1 : span].astype(jnp.float32)
                    if has_nearer:
                        shade = shade + nearer_ref[z, at, :]
                    base = base + emitted
                    lit = lit + emitted * jnp.exp2(shade * light_scale)
                outs.append((base, lit, before))
            for channel in range(3):
                for pair in range(shares // 2):
                    halves = []
                    for side in range(2):
                        first = (2 * pair + side) * share_rows
                        halves.append(jnp.concatenate([o[channel][first : first + share_rows] for o in outs], axis=0))
                    to = (step * group + g) * (shares // 2) + pair
                    keep_ref[channel, to] = jnp.where(odd, halves[1], halves[0])
                    give_ref[channel, to] = jnp.where(odd, halves[0], halves[1])
        return carry

    lax.fori_loop(0, rows // tall, work, 0)


def composite_slab(clip_flags, density, nearer, kappa, extinct, depth_n):
    slices, rows, cells = density.shape
    share_rows = rows // depth_n
    blocks_r, blocks_x = clip_flags.shape[1:]
    half = (3, depth_n // 2, share_rows * cells // LANES, LANES)
    log2e = math.log2(math.e)
    has_nearer = nearer is not None
    span = math.gcd(cells, 2 * LANES)
    tall = math.gcd(blocks_r, 2) * rows // blocks_r
    vmem = pl.BlockSpec(memory_space=pltpu.VMEM)
    return pl.pallas_call(
        functools.partial(slab_kernel, -kappa * log2e, -extinct * log2e, share_rows, has_nearer),
        out_shape=[jax.ShapeDtypeStruct(half, jnp.float32)] * 2,
        in_specs=[pl.BlockSpec(memory_space=pltpu.HBM)] * 2 + [vmem] * has_nearer,
        out_specs=[vmem, vmem],
        scratch_shapes=[
            pltpu.VMEM((slices, rows, cells), jnp.bfloat16),
            pltpu.VMEM((cells // span, slices, tall, span), jnp.bfloat16),
            pltpu.VMEM((cells // span, slices, tall, span), jnp.float32),
            pltpu.VMEM((span, span), jnp.bfloat16),
            pltpu.SMEM((blocks_r, blocks_x, slices), jnp.int32),
            pltpu.SemaphoreType.DMA((rows // tall,)),
            pltpu.SemaphoreType.DMA,
        ],
        compiler_params=pltpu.CompilerParams(vmem_limit_bytes=60 * 2**20),
        cost_estimate=pl.CostEstimate(
            flops=2 * slices * rows * cells * cells,
            bytes_accessed=2 * slices * rows * cells,
            transcendentals=2 * slices * rows * cells,
        ),
        name="slab",
    )(clip_flags.transpose(1, 2, 0), density, *([nearer] if has_nearer else []))


def exchange(pieces, my_slab, my_rank, low, kappa):
    depth_n = lax.axis_size("depth")
    held = [pieces[0]]
    for m in range(1, len(pieces)):
        pairs = [(source, source ^ (m << low)) for source in range(depth_n)]
        held.append(lax.ppermute(pieces[m], "depth", pairs))
    place = my_rank >> low & (len(pieces) - 1)
    colors = 0.0
    for m, piece in enumerate(held):
        ahead = 0.0
        for other, front in enumerate(held):
            if other != m:
                ahead = ahead + front[2] * ((place ^ other) < (place ^ m)).astype(jnp.float32)
        colors = colors + piece[:2] * jnp.exp(-kappa * ahead)[None]
    return jnp.concatenate([colors, sum(piece[2:] for piece in held)], axis=0)


def on_device(density, clip_flags, band_offset, order, ambient, diffuse):
    slices, rows, cells = density.shape
    depth_n = lax.axis_size("depth")
    xs_n = lax.axis_size("xs")
    kappa = 2.0 / (slices * depth_n)
    extinct = 2.0 / (cells * xs_n)
    share_rows = rows // depth_n
    levels = depth_n.bit_length() - 1
    my_slab = lax.axis_index("depth")
    my_rank = my_slab ^ order[0]
    nearer = None
    if xs_n > 1:
        blocks_r, blocks_x = clip_flags.shape[1:]
        kept = density.astype(jnp.float32).reshape(
            slices, blocks_r, rows // blocks_r, blocks_x, cells // blocks_x
        )
        totals = jnp.sum(kept, axis=4) * clip_flags[:, :, None, :].astype(jnp.float32)
        totals = jnp.sum(totals, axis=3).reshape(slices, rows)
        nearer = prefix(totals, "xs", lambda early, late: early + late, jnp.zeros_like(totals))
        nearer = nearer[:, :, None]
    pieces = composite_slab(clip_flags, density, nearer, kappa, extinct, depth_n)
    share = exchange(pieces, my_slab, my_rank, 0, kappa)
    low = 1
    while low < levels:
        count = 4 if low + 1 < levels else 2
        split = share.reshape(3, share.shape[1] // count, count, *share.shape[2:])
        mine = my_slab >> low & (count - 1)
        pieces = [
            lax.dynamic_index_in_dim(split, mine ^ m, axis=2, keepdims=False) for m in range(count)
        ]
        share = exchange(pieces, my_slab, my_rank, low, kappa)
        low += count.bit_length() - 1
    share = share.reshape(3, cells // LANES, share_rows, LANES)
    share = share.transpose(0, 2, 1, 3).reshape(3, share_rows, cells)
    row_pos = band_offset[0] + my_slab * share_rows + jnp.arange(share_rows, dtype=jnp.int32)
    source = 0.6 + 0.4 * jnp.cos(2.0 * math.pi * row_pos.astype(jnp.float32) / 64.0)
    lit = source[:, None] * share[1]
    colors = ambient[:, None, None] * share[0][None] + diffuse[:, None, None] * lit[None]
    alpha = -jnp.expm1(-kappa * share[2])
    return jnp.concatenate([colors, alpha[None]], axis=0)


def solution(mesh):
    return jax.shard_map(
        on_device,
        mesh=mesh,
        in_specs=(P("depth", None, "xs"), P("depth", None, "xs"), P(), P(), P(), P()),
        out_specs=P(None, "depth", "xs"),
        check_vma=False,
    )
```

```python
import functools
import math

import jax
import jax.numpy as jnp
from jax import lax
from jax.experimental import pallas as pl
from jax.experimental.pallas import tpu as pltpu

from jax.sharding import PartitionSpec as P

LANES = 128

def prefix(value, axis, join, neutral):
    count, mine = (lax.axis_size(axis), lax.axis_index(axis))
    pieces = lax.all_gather(value, axis)
    so_far = jnp.full_like(value, 0) + jnp.asarray(neutral, value.dtype)

    def lap(position, so_far):
        longer = join(so_far, pieces[position])
        return jnp.where(position < mine, longer, so_far)

    return lax.fori_loop(0, count - 1, lap, so_far)


def slab_kernel(depth_scale, light_scale, share_rows, has_nearer, flags_hbm, dens_ref, *rest):
    if has_nearer:
        nearer_ref, *rest = rest
    keep_ref, give_ref, dens, masked, inside, upper, flags, sems, flag_sem = rest
    slices, rows, cells = dens.shape
    blocks_r, blocks_x = flags.shape[:2]
    band = rows // blocks_r
    width = cells // blocks_x
    span = upper.shape[0]
    group = masked.shape[2] // band
    tall = group * band
    shares = band // share_rows

    def copy(step):
        at = pl.ds(pl.multiple_of(step * tall, tall), tall)
        return pltpu.make_async_copy(dens_ref.at[:, at, :], dens.at[:, at, :], sems.at[step])

    flag_copy = pltpu.make_async_copy(flags_hbm, flags, flag_sem)
    flag_copy.start()
    for step in range(rows // tall):
        copy(step).start()
    upper[...] = (
        lax.broadcasted_iota(jnp.int32, (span, span), 0) < lax.broadcasted_iota(jnp.int32, (span, span), 1)
    ).astype(jnp.float32).astype(jnp.bfloat16)
    odd = lax.axis_index("depth") & 1 == 1
    flag_copy.wait()

    def work(step, carry):
        copy(step).wait()
        for g in range(group):
            block = step * group + g
            at = pl.ds(pl.multiple_of(block * band, band), band)
            for j in range(blocks_x):
                for z in range(slices):
                    flag = flags[block, j, z].astype(jnp.float32)
                    flag = jnp.full((band, width), flag, jnp.float32).astype(jnp.bfloat16)
                    masked[j * width // span, z, g * band : (g + 1) * band, j * width % span : j * width % span + width] = (
                        dens[z, at, j * width : (j + 1) * width] * flag
                    )
        lhs = masked[...].reshape(cells // span * slices * tall, span)
        inside[...] = jnp.dot(lhs, upper[...], preferred_element_type=jnp.float32).reshape(inside.shape)
        for g in range(group):
            sub = slice(g * band, (g + 1) * band)
            at = pl.ds(pl.multiple_of((step * group + g) * band, band), band)
            outs = []
            for j in range(cells // LANES):
                h, first = j * LANES // span, j * LANES % span
                cols = slice(first, first + LANES)
                before = jnp.zeros((band, LANES), jnp.float32)
                through = jnp.ones((band, LANES), jnp.float32)
                base = jnp.zeros((band, LANES), jnp.float32)
                lit = jnp.zeros((band, LANES), jnp.float32)
                for z in range(slices):
                    clipped = masked[h, z, sub, cols].astype(jnp.float32)
                    before = before + clipped
                    behind = jnp.exp2(before * depth_scale)
                    emitted = clipped * (through - behind)
                    through = behind
                    shade = inside[h, z, sub, cols]
                    for left in range(h):
                        shade = shade + inside[left, z, sub, span - 1 : span] + masked[left, z, sub, span - 1 : span].astype(jnp.float32)
                    if has_nearer:
                        shade = shade + nearer_ref[z, at, :]
                    base = base + emitted
                    lit = lit + emitted * jnp.exp2(shade * light_scale)
                outs.append((base, lit, before))
            for channel in range(3):
                for pair in range(shares // 2):
                    halves = []
                    for side in range(2):
                        first = (2 * pair + side) * share_rows
                        halves.append(jnp.concatenate([o[channel][first : first + share_rows] for o in outs], axis=0))
                    to = (step * group + g) * (shares // 2) + pair
                    keep_ref[channel, to] = jnp.where(odd, halves[1], halves[0])
                    give_ref[channel, to] = jnp.where(odd, halves[0], halves[1])
        return carry

    lax.fori_loop(0, rows // tall, work, 0)


def composite_slab(clip_flags, density, nearer, kappa, extinct, depth_n):
    slices, rows, cells = density.shape
    share_rows = rows // depth_n
    blocks_r, blocks_x = clip_flags.shape[1:]
    half = (3, depth_n // 2, share_rows * cells // LANES, LANES)
    log2e = math.log2(math.e)
    has_nearer = nearer is not None
    span = math.gcd(cells, 2 * LANES)
    tall = math.gcd(blocks_r, 2) * rows // blocks_r
    vmem = pl.BlockSpec(memory_space=pltpu.VMEM)
    return pl.pallas_call(
        functools.partial(slab_kernel, -kappa * log2e, -extinct * log2e, share_rows, has_nearer),
        out_shape=[pltpu.VMEM(half, jnp.float32)] * 2,
        in_specs=[pl.BlockSpec(memory_space=pltpu.HBM)] * 2 + [vmem] * has_nearer,
        out_specs=[vmem, vmem],
        scratch_shapes=[
            pltpu.VMEM((slices, rows, cells), jnp.bfloat16),
            pltpu.VMEM((cells // span, slices, tall, span), jnp.bfloat16),
            pltpu.VMEM((cells // span, slices, tall, span), jnp.float32),
            pltpu.VMEM((span, span), jnp.bfloat16),
            pltpu.SMEM((blocks_r, blocks_x, slices), jnp.int32),
            pltpu.SemaphoreType.DMA((rows // tall,)),
            pltpu.SemaphoreType.DMA,
        ],
        compiler_params=pltpu.CompilerParams(vmem_limit_bytes=24 * 2**20),
        cost_estimate=pl.CostEstimate(
            flops=2 * slices * rows * cells * cells,
            bytes_accessed=2 * slices * rows * cells,
            transcendentals=2 * slices * rows * cells,
        ),
        name="slab",
    )(clip_flags.transpose(1, 2, 0), pltpu.with_memory_space_constraint(density, pltpu.HBM), *([nearer] if has_nearer else []))


def exchange(pieces, my_slab, my_rank, low, kappa):
    depth_n = lax.axis_size("depth")
    held = [pieces[0]]
    for m in range(1, len(pieces)):
        pairs = [(source, source ^ (m << low)) for source in range(depth_n)]
        held.append(lax.ppermute(pieces[m], "depth", pairs))
    place = my_rank >> low & (len(pieces) - 1)
    colors = 0.0
    for m, piece in enumerate(held):
        ahead = 0.0
        for other, front in enumerate(held):
            if other != m:
                ahead = ahead + front[2] * ((place ^ other) < (place ^ m)).astype(jnp.float32)
        colors = colors + piece[:2] * jnp.exp(-kappa * ahead)[None]
    return jnp.concatenate([colors, sum(piece[2:] for piece in held)], axis=0)


def on_device(density, clip_flags, band_offset, order, ambient, diffuse):
    slices, rows, cells = density.shape
    depth_n = lax.axis_size("depth")
    xs_n = lax.axis_size("xs")
    kappa = 2.0 / (slices * depth_n)
    extinct = 2.0 / (cells * xs_n)
    share_rows = rows // depth_n
    levels = depth_n.bit_length() - 1
    my_slab = lax.axis_index("depth")
    my_rank = my_slab ^ order[0]
    nearer = None
    if xs_n > 1:
        blocks_r, blocks_x = clip_flags.shape[1:]
        kept = density.astype(jnp.float32).reshape(
            slices, blocks_r, rows // blocks_r, blocks_x, cells // blocks_x
        )
        totals = jnp.sum(kept, axis=4) * clip_flags[:, :, None, :].astype(jnp.float32)
        totals = jnp.sum(totals, axis=3).reshape(slices, rows)
        nearer = prefix(totals, "xs", lambda early, late: early + late, jnp.zeros_like(totals))
        nearer = nearer[:, :, None]
    pieces = composite_slab(clip_flags, density, nearer, kappa, extinct, depth_n)
    share = exchange(pieces, my_slab, my_rank, 0, kappa)
    low = 1
    while low < levels:
        count = 4 if low + 1 < levels else 2
        split = share.reshape(3, share.shape[1] // count, count, *share.shape[2:])
        mine = my_slab >> low & (count - 1)
        pieces = [
            lax.dynamic_index_in_dim(split, mine ^ m, axis=2, keepdims=False) for m in range(count)
        ]
        share = exchange(pieces, my_slab, my_rank, low, kappa)
        low += count.bit_length() - 1
    share = share.reshape(3, cells // LANES, share_rows, LANES)
    share = share.transpose(0, 2, 1, 3).reshape(3, share_rows, cells)
    row_pos = band_offset[0] + my_slab * share_rows + jnp.arange(share_rows, dtype=jnp.int32)
    source = 0.6 + 0.4 * jnp.cos(2.0 * math.pi * row_pos.astype(jnp.float32) / 64.0)
    lit = source[:, None] * share[1]
    colors = ambient[:, None, None] * share[0][None] + diffuse[:, None, None] * lit[None]
    alpha = -jnp.expm1(-kappa * share[2])
    return jnp.concatenate([colors, alpha[None]], axis=0)


def solution(mesh):
    return jax.shard_map(
        on_device,
        mesh=mesh,
        in_specs=(P("depth", None, "xs"), P("depth", None, "xs"), P(), P(), P(), P()),
        out_specs=P(None, "depth", "xs"),
        check_vma=False,
    )
```

```python
import functools
import math

import jax
import jax.numpy as jnp
from jax import lax
from jax.experimental import pallas as pl
from jax.experimental.pallas import tpu as pltpu

from jax.sharding import PartitionSpec as P

LANES = 128

def prefix(value, axis, join, neutral):
    count, mine = (lax.axis_size(axis), lax.axis_index(axis))
    pieces = lax.all_gather(value, axis)
    so_far = jnp.full_like(value, 0) + jnp.asarray(neutral, value.dtype)

    def lap(position, so_far):
        longer = join(so_far, pieces[position])
        return jnp.where(position < mine, longer, so_far)

    return lax.fori_loop(0, count - 1, lap, so_far)


def slab_kernel(depth_scale, light_scale, share_rows, has_nearer, flags_hbm, dens_ref, *rest):
    if has_nearer:
        nearer_ref, *rest = rest
    keep_ref, give_ref, dens, masked, inside, upper, flags, sems, flag_sem = rest
    slices, rows, cells = dens.shape
    blocks_r, blocks_x = flags.shape[:2]
    band = rows // blocks_r
    width = cells // blocks_x
    span = upper.shape[0]
    group = masked.shape[2] // band
    tall = group * band
    shares = band // share_rows

    def copy(step):
        at = pl.ds(pl.multiple_of(step * tall, tall), tall)
        return pltpu.make_async_copy(dens_ref.at[:, at, :], dens.at[:, at, :], sems.at[step])

    flag_copy = pltpu.make_async_copy(flags_hbm, flags, flag_sem)
    flag_copy.start()
    for step in range(rows // tall):
        copy(step).start()
    upper[...] = (
        lax.broadcasted_iota(jnp.int32, (span, span), 0) < lax.broadcasted_iota(jnp.int32, (span, span), 1)
    ).astype(jnp.float32).astype(jnp.bfloat16)
    odd = lax.axis_index("depth") & 1 == 1
    flag_copy.wait()

    def work(step, carry):
        copy(step).wait()
        for g in range(group):
            block = step * group + g
            at = pl.ds(pl.multiple_of(block * band, band), band)
            for j in range(blocks_x):
                for z in range(slices):
                    flag = flags[block, j, z].astype(jnp.float32)
                    flag = jnp.full((band, width), flag, jnp.float32).astype(jnp.bfloat16)
                    masked[j * width // span, z, g * band : (g + 1) * band, j * width % span : j * width % span + width] = (
                        dens[z, at, j * width : (j + 1) * width] * flag
                    )
        lhs = masked[...].reshape(cells // span * slices * tall, span)
        inside[...] = jnp.dot(lhs, upper[...], preferred_element_type=jnp.float32).reshape(inside.shape)
        for g in range(group):
            sub = slice(g * band, (g + 1) * band)
            at = pl.ds(pl.multiple_of((step * group + g) * band, band), band)
            outs = []
            for j in range(cells // LANES):
                h, first = j * LANES // span, j * LANES % span
                cols = slice(first, first + LANES)
                before = jnp.zeros((band, LANES), jnp.float32)
                through = jnp.ones((band, LANES), jnp.float32)
                base = jnp.zeros((band, LANES), jnp.float32)
                lit = jnp.zeros((band, LANES), jnp.float32)
                for z in range(slices):
                    clipped = masked[h, z, sub, cols].astype(jnp.float32)
                    before = before + clipped
                    behind = jnp.exp2(before * depth_scale)
                    emitted = clipped * (through - behind)
                    through = behind
                    shade = inside[h, z, sub, cols]
                    for left in range(h):
                        shade = shade + inside[left, z, sub, span - 1 : span] + masked[left, z, sub, span - 1 : span].astype(jnp.float32)
                    if has_nearer:
                        shade = shade + nearer_ref[z, at, :]
                    base = base + emitted
                    lit = lit + emitted * jnp.exp2(shade * light_scale)
                outs.append((base, lit, before))
            for channel in range(3):
                for pair in range(shares // 2):
                    halves = []
                    for side in range(2):
                        first = (2 * pair + side) * share_rows
                        halves.append(jnp.concatenate([o[channel][first : first + share_rows] for o in outs], axis=0))
                    to = (step * group + g) * (shares // 2) + pair
                    keep_ref[channel, to] = jnp.where(odd, halves[1], halves[0])
                    give_ref[channel, to] = jnp.where(odd, halves[0], halves[1])
        return carry

    lax.fori_loop(0, rows // tall, work, 0)


def composite_slab(clip_flags, density, nearer, kappa, extinct, depth_n):
    slices, rows, cells = density.shape
    share_rows = rows // depth_n
    blocks_r, blocks_x = clip_flags.shape[1:]
    half = (3, depth_n // 2, share_rows * cells // LANES, LANES)
    log2e = math.log2(math.e)
    has_nearer = nearer is not None
    span = math.gcd(cells, 2 * LANES)
    tall = math.gcd(blocks_r, 2) * rows // blocks_r
    vmem = pl.BlockSpec(memory_space=pltpu.VMEM)
    return pl.pallas_call(
        functools.partial(slab_kernel, -kappa * log2e, -extinct * log2e, share_rows, has_nearer),
        out_shape=[pltpu.VMEM(half, jnp.float32)] * 2,
        in_specs=[pl.BlockSpec(memory_space=pltpu.HBM)] * 2 + [vmem] * has_nearer,
        out_specs=[vmem, vmem],
        scratch_shapes=[
            pltpu.VMEM((slices, rows, cells), jnp.bfloat16),
            pltpu.VMEM((cells // span, slices, tall, span), jnp.bfloat16),
            pltpu.VMEM((cells // span, slices, tall, span), jnp.float32),
            pltpu.VMEM((span, span), jnp.bfloat16),
            pltpu.SMEM((blocks_r, blocks_x, slices), jnp.int32),
            pltpu.SemaphoreType.DMA((rows // tall,)),
            pltpu.SemaphoreType.DMA,
        ],
        compiler_params=pltpu.CompilerParams(vmem_limit_bytes=24 * 2**20),
        cost_estimate=pl.CostEstimate(
            flops=2 * slices * rows * cells * cells,
            bytes_accessed=2 * slices * rows * cells,
            transcendentals=2 * slices * rows * cells,
        ),
        name="slab",
    )(clip_flags.transpose(1, 2, 0), pltpu.with_memory_space_constraint(density, pltpu.HBM), *([nearer] if has_nearer else []))


def exchange(pieces, my_slab, my_rank, low, kappa):
    depth_n = lax.axis_size("depth")
    held = {0: pieces[0]}
    for m in range(len(pieces) - 1, 0, -1):
        pairs = [(source, source ^ (m << low)) for source in range(depth_n)]
        held[m] = lax.ppermute(pieces[m], "depth", pairs)
    place = my_rank >> low & (len(pieces) - 1)
    colors = 0.0
    for m, piece in held.items():
        ahead = 0.0
        for other, front in held.items():
            if other != m:
                ahead = ahead + front[2] * ((place ^ other) < (place ^ m)).astype(jnp.float32)
        colors = colors + piece[:2] * jnp.exp(-kappa * ahead)[None]
    return jnp.concatenate([colors, sum(piece[2:] for piece in held.values())], axis=0)


def on_device(density, clip_flags, band_offset, order, ambient, diffuse):
    slices, rows, cells = density.shape
    depth_n = lax.axis_size("depth")
    xs_n = lax.axis_size("xs")
    kappa = 2.0 / (slices * depth_n)
    extinct = 2.0 / (cells * xs_n)
    share_rows = rows // depth_n
    levels = depth_n.bit_length() - 1
    my_slab = lax.axis_index("depth")
    my_rank = my_slab ^ order[0]
    nearer = None
    if xs_n > 1:
        blocks_r, blocks_x = clip_flags.shape[1:]
        kept = density.astype(jnp.float32).reshape(
            slices, blocks_r, rows // blocks_r, blocks_x, cells // blocks_x
        )
        totals = jnp.sum(kept, axis=4) * clip_flags[:, :, None, :].astype(jnp.float32)
        totals = jnp.sum(totals, axis=3).reshape(slices, rows)
        nearer = prefix(totals, "xs", lambda early, late: early + late, jnp.zeros_like(totals))
        nearer = nearer[:, :, None]
    pieces = composite_slab(clip_flags, density, nearer, kappa, extinct, depth_n)
    share = exchange(pieces, my_slab, my_rank, 0, kappa)
    low = 1
    while low < levels:
        count = 4 if low + 1 < levels else 2
        split = share.reshape(3, share.shape[1] // count, count, *share.shape[2:])
        mine = my_slab >> low & (count - 1)
        pieces = [
            lax.dynamic_index_in_dim(split, mine ^ m, axis=2, keepdims=False) for m in range(count)
        ]
        share = exchange(pieces, my_slab, my_rank, low, kappa)
        low += count.bit_length() - 1
    share = share.reshape(3, cells // LANES, share_rows, LANES)
    share = share.transpose(0, 2, 1, 3).reshape(3, share_rows, cells)
    row_pos = band_offset[0] + my_slab * share_rows + jnp.arange(share_rows, dtype=jnp.int32)
    source = 0.6 + 0.4 * jnp.cos(2.0 * math.pi * row_pos.astype(jnp.float32) / 64.0)
    lit = source[:, None] * share[1]
    colors = ambient[:, None, None] * share[0][None] + diffuse[:, None, None] * lit[None]
    alpha = -jnp.expm1(-kappa * share[2])
    return jnp.concatenate([colors, alpha[None]], axis=0)


def solution(mesh):
    return jax.shard_map(
        on_device,
        mesh=mesh,
        in_specs=(P("depth", None, "xs"), P("depth", None, "xs"), P(), P(), P(), P()),
        out_specs=P(None, "depth", "xs"),
        check_vma=False,
    )
```

```python
import functools
import math

import jax
import jax.numpy as jnp
from jax import lax
from jax.experimental import pallas as pl
from jax.experimental.pallas import tpu as pltpu

from jax.sharding import PartitionSpec as P

LANES = 128

def prefix(value, axis, join, neutral):
    count, mine = (lax.axis_size(axis), lax.axis_index(axis))
    pieces = lax.all_gather(value, axis)
    so_far = jnp.full_like(value, 0) + jnp.asarray(neutral, value.dtype)

    def lap(position, so_far):
        longer = join(so_far, pieces[position])
        return jnp.where(position < mine, longer, so_far)

    return lax.fori_loop(0, count - 1, lap, so_far)


def slab_kernel(depth_scale, light_scale, share_rows, has_nearer, flags_hbm, dens_ref, *rest):
    if has_nearer:
        nearer_ref, *rest = rest
    keep_ref, give_ref, dens, masked, inside, upper, flags, sems, flag_sem = rest
    slices, rows, cells = dens.shape
    blocks_r, blocks_x = flags.shape[:2]
    band = rows // blocks_r
    width = cells // blocks_x
    span = math.gcd(cells, 2 * LANES)
    group = masked.shape[1] // band
    tall = group * band
    shares = band // share_rows

    def copy(step):
        at = pl.ds(pl.multiple_of(step * tall, tall), tall)
        return pltpu.make_async_copy(dens_ref.at[:, at, :], dens.at[:, at, :], sems.at[step])

    flag_copy = pltpu.make_async_copy(flags_hbm, flags, flag_sem)
    flag_copy.start()
    for step in range(rows // tall):
        copy(step).start()
    upper[...] = (
        lax.broadcasted_iota(jnp.int32, (cells, cells), 0) < lax.broadcasted_iota(jnp.int32, (cells, cells), 1)
    ).astype(jnp.float32).astype(jnp.bfloat16)
    odd = lax.axis_index("depth") & 1 == 1
    flag_copy.wait()

    def work(step, carry):
        copy(step).wait()
        for g in range(group):
            block = step * group + g
            at = pl.ds(pl.multiple_of(block * band, band), band)
            for j in range(blocks_x):
                for z in range(slices):
                    flag = flags[block, j, z].astype(jnp.float32)
                    flag = jnp.full((band, width), flag, jnp.float32).astype(jnp.bfloat16)
                    cols = slice(j * width, (j + 1) * width)
                    masked[z, g * band : (g + 1) * band, cols] = dens[z, at, cols] * flag
        for h in range(cells // span):
            lhs = masked[:, :, : (h + 1) * span].reshape(slices * tall, (h + 1) * span)
            cols = slice(h * span, (h + 1) * span)
            inside[:, :, cols] = jnp.dot(
                lhs, upper[: (h + 1) * span, cols], preferred_element_type=jnp.float32
            ).reshape(slices, tall, span)
        for g in range(group):
            sub = slice(g * band, (g + 1) * band)
            at = pl.ds(pl.multiple_of((step * group + g) * band, band), band)
            outs = []
            for j in range(cells // LANES):
                cols = slice(j * LANES, (j + 1) * LANES)
                before = jnp.zeros((band, LANES), jnp.float32)
                through = jnp.ones((band, LANES), jnp.float32)
                base = jnp.zeros((band, LANES), jnp.float32)
                lit = jnp.zeros((band, LANES), jnp.float32)
                for z in range(slices):
                    clipped = masked[z, sub, cols].astype(jnp.float32)
                    before = before + clipped
                    behind = jnp.exp2(before * depth_scale)
                    emitted = clipped * (through - behind)
                    through = behind
                    shade = inside[z, sub, cols]
                    if has_nearer:
                        shade = shade + nearer_ref[z, at, :]
                    base = base + emitted
                    lit = lit + emitted * jnp.exp2(shade * light_scale)
                outs.append((base, lit, before))
            for channel in range(3):
                for pair in range(shares // 2):
                    halves = []
                    for side in range(2):
                        first = (2 * pair + side) * share_rows
                        halves.append(jnp.concatenate([o[channel][first : first + share_rows] for o in outs], axis=0))
                    to = (step * group + g) * (shares // 2) + pair
                    keep_ref[channel, to] = jnp.where(odd, halves[1], halves[0])
                    give_ref[channel, to] = jnp.where(odd, halves[0], halves[1])
        return carry

    lax.fori_loop(0, rows // tall, work, 0)


def composite_slab(clip_flags, density, nearer, kappa, extinct, depth_n):
    slices, rows, cells = density.shape
    share_rows = rows // depth_n
    blocks_r, blocks_x = clip_flags.shape[1:]
    half = (3, depth_n // 2, share_rows * cells // LANES, LANES)
    log2e = math.log2(math.e)
    has_nearer = nearer is not None
    tall = math.gcd(blocks_r, 2) * rows // blocks_r
    vmem = pl.BlockSpec(memory_space=pltpu.VMEM)
    return pl.pallas_call(
        functools.partial(slab_kernel, -kappa * log2e, -extinct * log2e, share_rows, has_nearer),
        out_shape=[pltpu.VMEM(half, jnp.float32)] * 2,
        in_specs=[pl.BlockSpec(memory_space=pltpu.HBM)] * 2 + [vmem] * has_nearer,
        out_specs=[vmem, vmem],
        scratch_shapes=[
            pltpu.VMEM((slices, rows, cells), jnp.bfloat16),
            pltpu.VMEM((slices, tall, cells), jnp.bfloat16),
            pltpu.VMEM((slices, tall, cells), jnp.float32),
            pltpu.VMEM((cells, cells), jnp.bfloat16),
            pltpu.SMEM((blocks_r, blocks_x, slices), jnp.int32),
            pltpu.SemaphoreType.DMA((rows // tall,)),
            pltpu.SemaphoreType.DMA,
        ],
        compiler_params=pltpu.CompilerParams(vmem_limit_bytes=24 * 2**20),
        cost_estimate=pl.CostEstimate(
            flops=2 * slices * rows * cells * cells,
            bytes_accessed=2 * slices * rows * cells,
            transcendentals=2 * slices * rows * cells,
        ),
        name="slab",
    )(pltpu.with_memory_space_constraint(clip_flags.transpose(1, 2, 0), pltpu.HBM), pltpu.with_memory_space_constraint(density, pltpu.HBM), *([nearer] if has_nearer else []))


def exchange(pieces, my_slab, my_rank, low, kappa):
    depth_n = lax.axis_size("depth")
    held = {0: pieces[0]}
    for m in range(len(pieces) - 1, 0, -1):
        pairs = [(source, source ^ (m << low)) for source in range(depth_n)]
        held[m] = lax.ppermute(pieces[m], "depth", pairs)
    place = my_rank >> low & (len(pieces) - 1)
    colors = 0.0
    for m, piece in held.items():
        ahead = 0.0
        for other, front in held.items():
            if other != m:
                ahead = ahead + front[2] * ((place ^ other) < (place ^ m)).astype(jnp.float32)
        colors = colors + piece[:2] * jnp.exp(-kappa * ahead)[None]
    return jnp.concatenate([colors, sum(piece[2:] for piece in held.values())], axis=0)


def on_device(density, clip_flags, band_offset, order, ambient, diffuse):
    slices, rows, cells = density.shape
    depth_n = lax.axis_size("depth")
    xs_n = lax.axis_size("xs")
    kappa = 2.0 / (slices * depth_n)
    extinct = 2.0 / (cells * xs_n)
    share_rows = rows // depth_n
    levels = depth_n.bit_length() - 1
    my_slab = lax.axis_index("depth")
    my_rank = my_slab ^ order[0]
    nearer = None
    if xs_n > 1:
        blocks_r, blocks_x = clip_flags.shape[1:]
        kept = density.astype(jnp.float32).reshape(
            slices, blocks_r, rows // blocks_r, blocks_x, cells // blocks_x
        )
        totals = jnp.sum(kept, axis=4) * clip_flags[:, :, None, :].astype(jnp.float32)
        totals = jnp.sum(totals, axis=3).reshape(slices, rows)
        nearer = prefix(totals, "xs", lambda early, late: early + late, jnp.zeros_like(totals))
        nearer = nearer[:, :, None]
    pieces = composite_slab(clip_flags, density, nearer, kappa, extinct, depth_n)
    share = exchange(pieces, my_slab, my_rank, 0, kappa)
    low = 1
    while low < levels:
        count = 4 if low + 1 < levels else 2
        split = share.reshape(3, share.shape[1] // count, count, *share.shape[2:])
        mine = my_slab >> low & (count - 1)
        pieces = [
            lax.dynamic_index_in_dim(split, mine ^ m, axis=2, keepdims=False) for m in range(count)
        ]
        share = exchange(pieces, my_slab, my_rank, low, kappa)
        low += count.bit_length() - 1
    share = share.reshape(3, cells // LANES, share_rows, LANES)
    share = share.transpose(0, 2, 1, 3).reshape(3, share_rows, cells)
    row_pos = band_offset[0] + my_slab * share_rows + jnp.arange(share_rows, dtype=jnp.int32)
    source = 0.6 + 0.4 * jnp.cos(2.0 * math.pi * row_pos.astype(jnp.float32) / 64.0)
    lit = source[:, None] * share[1]
    colors = ambient[:, None, None] * share[0][None] + diffuse[:, None, None] * lit[None]
    alpha = -jnp.expm1(-kappa * share[2])
    return jnp.concatenate([colors, alpha[None]], axis=0)


def solution(mesh):
    return jax.shard_map(
        on_device,
        mesh=mesh,
        in_specs=(P("depth", None, "xs"), P("depth", None, "xs"), P(), P(), P(), P()),
        out_specs=P(None, "depth", "xs"),
        check_vma=False,
    )
```

```python
import functools
import math

import jax
import jax.numpy as jnp
from jax import lax
from jax.experimental import pallas as pl
from jax.experimental.pallas import tpu as pltpu

from jax.sharding import PartitionSpec as P

LANES = 128

def prefix(value, axis, join, neutral):
    count, mine = (lax.axis_size(axis), lax.axis_index(axis))
    pieces = lax.all_gather(value, axis)
    so_far = jnp.full_like(value, 0) + jnp.asarray(neutral, value.dtype)

    def lap(position, so_far):
        longer = join(so_far, pieces[position])
        return jnp.where(position < mine, longer, so_far)

    return lax.fori_loop(0, count - 1, lap, so_far)


def slab_kernel(depth_scale, light_scale, share_rows, has_nearer, flags_hbm, dens_ref, *rest):
    if has_nearer:
        nearer_ref, *rest = rest
    keep_ref, give_ref, dens, masked, inside, upper, flags, sems, flag_sem = rest
    slices, rows, cells = dens.shape
    blocks_r, blocks_x = flags.shape[:2]
    band = rows // blocks_r
    width = cells // blocks_x
    span = math.gcd(cells, 2 * LANES)
    group = masked.shape[1] // band
    tall = group * band
    shares = band // share_rows

    def copy(step):
        at = pl.ds(pl.multiple_of(step * tall, tall), tall)
        return pltpu.make_async_copy(dens_ref.at[:, at, :], dens.at[:, at, :], sems.at[step])

    flag_copy = pltpu.make_async_copy(flags_hbm, flags, flag_sem)
    flag_copy.start()
    for step in range(rows // tall):
        copy(step).start()
    upper[...] = (
        lax.broadcasted_iota(jnp.int32, (cells, cells), 0) < lax.broadcasted_iota(jnp.int32, (cells, cells), 1)
    ).astype(jnp.float32).astype(jnp.bfloat16)
    odd = lax.axis_index("depth") & 1 == 1
    flag_copy.wait()

    def work(step, carry):
        copy(step).wait()
        for g in range(group):
            block = step * group + g
            at = pl.ds(pl.multiple_of(block * band, band), band)
            for j in range(blocks_x):
                for z in range(slices):
                    flag = flags[block, j, z].astype(jnp.float32)
                    flag = jnp.full((band, width), flag, jnp.float32).astype(jnp.bfloat16)
                    cols = slice(j * width, (j + 1) * width)
                    masked[z, g * band : (g + 1) * band, cols] = dens[z, at, cols] * flag
        for h in range(cells // span):
            lhs = masked[:, :, : (h + 1) * span].reshape(slices * tall, (h + 1) * span)
            cols = slice(h * span, (h + 1) * span)
            inside[:, :, cols] = jnp.dot(
                lhs, upper[: (h + 1) * span, cols], preferred_element_type=jnp.float32
            ).reshape(slices, tall, span)
        for g in range(group):
            sub = slice(g * band, (g + 1) * band)
            at = pl.ds(pl.multiple_of((step * group + g) * band, band), band)
            outs = []
            for j in range(cells // LANES):
                cols = slice(j * LANES, (j + 1) * LANES)
                before = jnp.zeros((band, LANES), jnp.float32)
                through = jnp.ones((band, LANES), jnp.float32)
                base = jnp.zeros((band, LANES), jnp.float32)
                lit = jnp.zeros((band, LANES), jnp.float32)
                for z in range(slices):
                    clipped = masked[z, sub, cols].astype(jnp.float32)
                    before = before + clipped
                    behind = jnp.exp2(before * depth_scale)
                    emitted = clipped * (through - behind)
                    through = behind
                    shade = inside[z, sub, cols]
                    if has_nearer:
                        shade = shade + nearer_ref[z, at, :]
                    base = base + emitted
                    lit = lit + emitted * jnp.exp2(shade * light_scale)
                outs.append((base, lit, before))
            for channel in range(3):
                for pair in range(shares // 2):
                    halves = []
                    for side in range(2):
                        first = (2 * pair + side) * share_rows
                        halves.append(jnp.concatenate([o[channel][first : first + share_rows] for o in outs], axis=0))
                    to = (step * group + g) * (shares // 2) + pair
                    keep_ref[channel, to] = jnp.where(odd, halves[1], halves[0])
                    give_ref[channel, to] = jnp.where(odd, halves[0], halves[1])
        return carry

    lax.fori_loop(0, rows // tall, work, 0)


def composite_slab(clip_flags, density, nearer, kappa, extinct, depth_n):
    slices, rows, cells = density.shape
    share_rows = rows // depth_n
    blocks_r, blocks_x = clip_flags.shape[1:]
    half = (3, depth_n // 2, share_rows * cells // LANES, LANES)
    log2e = math.log2(math.e)
    has_nearer = nearer is not None
    tall = math.gcd(blocks_r, 2) * rows // blocks_r
    vmem = pl.BlockSpec(memory_space=pltpu.VMEM)
    return pl.pallas_call(
        functools.partial(slab_kernel, -kappa * log2e, -extinct * log2e, share_rows, has_nearer),
        out_shape=[pltpu.VMEM(half, jnp.float32)] * 2,
        in_specs=[pl.BlockSpec(memory_space=pltpu.HBM)] * 2 + [vmem] * has_nearer,
        out_specs=[vmem, vmem],
        scratch_shapes=[
            pltpu.VMEM((slices, rows, cells), jnp.bfloat16),
            pltpu.VMEM((slices, tall, cells), jnp.bfloat16),
            pltpu.VMEM((slices, tall, cells), jnp.float32),
            pltpu.VMEM((cells, cells), jnp.bfloat16),
            pltpu.SMEM((blocks_r, blocks_x, slices), jnp.int32),
            pltpu.SemaphoreType.DMA((rows // tall,)),
            pltpu.SemaphoreType.DMA,
        ],
        compiler_params=pltpu.CompilerParams(vmem_limit_bytes=24 * 2**20),
        cost_estimate=pl.CostEstimate(
            flops=2 * slices * rows * cells * cells,
            bytes_accessed=2 * slices * rows * cells,
            transcendentals=2 * slices * rows * cells,
        ),
        name="slab",
    )(
        pltpu.with_memory_space_constraint(clip_flags.transpose(1, 2, 0), pltpu.HBM),
        pltpu.with_memory_space_constraint(density, pltpu.HBM),
        *([nearer] if has_nearer else []),
    )


def step_of(position, hop, count, ring):
    if ring:
        turn = ((position & 1) << 1 | position >> 1) + hop & 3
        return (turn & 1) << 1 | turn >> 1
    return position ^ hop


def sending_order(count, ring):
    if count < 4:
        return (1,)
    return (1, 3, 2) if ring else (3, 2, 1)


def sent_and_held(pieces, low, ring):
    depth_n = lax.axis_size("depth")
    count = len(pieces)
    held = []
    for hop in sending_order(count, ring):
        pairs = []
        for source in range(depth_n):
            position = source >> low & (count - 1)
            pairs.append((source, source + ((step_of(position, hop, count, ring) - position) << low)))
        held.append(lax.ppermute(pieces[hop], "depth", pairs))
    return [*held, pieces[0]]


def over(kappa, places, held):
    base, lit, column = 0.0, 0.0, 0.0
    for place, piece in zip(places, held):
        ahead = 0.0
        for other, front in zip(places, held):
            if front is not piece:
                ahead = ahead + jnp.where(other < place, front[2], 0.0)
        passed = jnp.exp(-kappa * ahead)
        base = base + piece[0] * passed
        lit = lit + piece[1] * passed
        column = column + piece[2]
    return base, lit, column


def places_of(order_ref, low, count, ring):
    mine = lax.axis_index("depth") >> low & (count - 1)
    flips = order_ref[0:1, 0:1] >> low & (count - 1)
    return [flips ^ step_of(mine, -hop if ring else hop, count, ring) for hop in (*sending_order(count, ring), 0)]


def merge_kernel(kappa, low, count, ring, next_ring, order_ref, *refs):
    held, out = refs[:count], refs[count:]
    places = places_of(order_ref, low, count, ring)
    fan = len(out)
    mine = lax.axis_index("depth") >> (low + count.bit_length() - 1) & (fan - 1)
    for hop in range(fan):
        for row in range(out[hop].shape[1]):
            at = row * fan + step_of(mine, hop, fan, next_ring)
            merged = over(kappa, places, [[piece[channel, at] for channel in range(3)] for piece in held])
            for channel in range(3):
                out[hop][channel, row] = merged[channel]


def opacity(depth):
    series = 1.0 - depth * (1.0 / 6.0)
    for term in (5.0, 4.0, 3.0, 2.0):
        series = 1.0 - depth * (1.0 / term) * series
    return jnp.where(depth < 0.125, depth * series, 1.0 - jnp.exp(-depth))


def finish_kernel(kappa, low, count, ring, order_ref, glow_ref, *refs):
    held, image = refs[:count], refs[count]
    places = places_of(order_ref, low, count, ring)
    base, lit, column = over(kappa, places, [[piece[channel, 0] for channel in range(3)] for piece in held])
    share_rows = image.shape[1]
    for channel in range(4):
        if channel < 3:
            value = glow_ref[0, channel] * base + glow_ref[1, channel] * lit
        else:
            value = opacity(kappa * column)
        for j in range(image.shape[2] // LANES):
            image[channel, :, j * LANES : (j + 1) * LANES] = value[j * share_rows : (j + 1) * share_rows]


def on_device(density, clip_flags, band_offset, order, ambient, diffuse):
    slices, rows, cells = density.shape
    depth_n = lax.axis_size("depth")
    xs_n = lax.axis_size("xs")
    kappa = 2.0 / (slices * depth_n)
    extinct = 2.0 / (cells * xs_n)
    share_rows = rows // depth_n
    levels = depth_n.bit_length() - 1
    my_slab = lax.axis_index("depth")
    nearer = None
    if xs_n > 1:
        blocks_r, blocks_x = clip_flags.shape[1:]
        kept = density.astype(jnp.float32).reshape(
            slices, blocks_r, rows // blocks_r, blocks_x, cells // blocks_x
        )
        totals = jnp.sum(kept, axis=4) * clip_flags[:, :, None, :].astype(jnp.float32)
        totals = jnp.sum(totals, axis=3).reshape(slices, rows)
        nearer = prefix(totals, "xs", lambda early, late: early + late, jnp.zeros_like(totals))
        nearer = nearer[:, :, None]
    held = sent_and_held(composite_slab(clip_flags, density, nearer, kappa, extinct, depth_n), 0, False)
    first = order[None]
    vmem = pl.BlockSpec(memory_space=pltpu.VMEM)
    low, ring = 0, False
    while True:
        count = len(held)
        through = low + count.bit_length() - 1
        if through == levels:
            break
        fan = 4 if through + 1 < levels else 2
        next_ring = low > 0 and fan == 4
        shape = (3, held[0].shape[1] // fan, *held[0].shape[2:])
        pieces = pl.pallas_call(
            functools.partial(merge_kernel, kappa, low, count, ring, next_ring),
            out_shape=[pltpu.VMEM(shape, jnp.float32)] * fan,
            in_specs=[vmem] * (1 + count),
            out_specs=[vmem] * fan,
            compiler_params=pltpu.CompilerParams(vmem_limit_bytes=4 * 2**20),
            name="merge",
        )(first, *held)
        low, ring = through, next_ring
        held = sent_and_held(pieces, low, ring)
    row_pos = band_offset[0] + my_slab * share_rows + jnp.arange(share_rows, dtype=jnp.int32)
    source = 0.6 + 0.4 * jnp.cos(2.0 * math.pi * row_pos.astype(jnp.float32) / 64.0)
    source = jnp.tile(source, cells // LANES)
    glow = jnp.stack([jnp.broadcast_to(ambient[:, None], (3, source.shape[0])), diffuse[:, None] * source[None]])
    glow = jnp.broadcast_to(glow[..., None], (*glow.shape, LANES))
    return pl.pallas_call(
        functools.partial(finish_kernel, kappa, low, len(held), ring),
        out_shape=jax.ShapeDtypeStruct((4, share_rows, cells), jnp.float32),
        in_specs=[vmem] * (2 + len(held)),
        compiler_params=pltpu.CompilerParams(vmem_limit_bytes=4 * 2**20),
        name="finish",
    )(first, glow, *held)


def solution(mesh):
    return jax.shard_map(
        on_device,
        mesh=mesh,
        in_specs=(P("depth", None, "xs"), P("depth", None, "xs"), P(), P(), P(), P()),
        out_specs=P(None, "depth", "xs"),
        check_vma=False,
    )
```

```python
import functools
import math

import jax
import jax.numpy as jnp
from jax import lax
from jax.experimental import pallas as pl
from jax.experimental.pallas import tpu as pltpu

from jax.sharding import PartitionSpec as P

LANES = 128

def prefix(value, axis, join, neutral):
    count, mine = (lax.axis_size(axis), lax.axis_index(axis))
    pieces = lax.all_gather(value, axis)
    so_far = jnp.full_like(value, 0) + jnp.asarray(neutral, value.dtype)

    def lap(position, so_far):
        longer = join(so_far, pieces[position])
        return jnp.where(position < mine, longer, so_far)

    return lax.fori_loop(0, count - 1, lap, so_far)


def slab_kernel(depth_scale, light_scale, share_rows, has_nearer, flags_hbm, dens_ref, *rest):
    if has_nearer:
        nearer_ref, *rest = rest
    keep_ref, give_ref, dens, masked, inside, upper, flags, sems, flag_sem = rest
    slices, rows, cells = dens.shape
    blocks_r, blocks_x = flags.shape[:2]
    band = rows // blocks_r
    width = cells // blocks_x
    span = math.gcd(cells, 2 * LANES)
    group = masked.shape[1] // band
    tall = group * band
    shares = band // share_rows

    def copy(step):
        at = pl.ds(pl.multiple_of(step * tall, tall), tall)
        return pltpu.make_async_copy(dens_ref.at[:, at, :], dens.at[:, at, :], sems.at[step])

    flag_copy = pltpu.make_async_copy(flags_hbm, flags, flag_sem)
    flag_copy.start()
    for step in range(rows // tall):
        copy(step).start()
    upper[...] = (
        lax.broadcasted_iota(jnp.int32, (cells, cells), 0) < lax.broadcasted_iota(jnp.int32, (cells, cells), 1)
    ).astype(jnp.float32).astype(jnp.bfloat16)
    odd = lax.axis_index("depth") & 1 == 1
    flag_copy.wait()

    def work(step, carry):
        copy(step).wait()
        for g in range(group):
            block = step * group + g
            at = pl.ds(pl.multiple_of(block * band, band), band)
            for j in range(blocks_x):
                for z in range(slices):
                    flag = flags[block, j, z].astype(jnp.float32)
                    flag = jnp.full((band, width), flag, jnp.float32).astype(jnp.bfloat16)
                    cols = slice(j * width, (j + 1) * width)
                    masked[z, g * band : (g + 1) * band, cols] = dens[z, at, cols] * flag
        for h in range(cells // span):
            lhs = masked[:, :, : (h + 1) * span].reshape(slices * tall, (h + 1) * span)
            cols = slice(h * span, (h + 1) * span)
            inside[:, :, cols] = jnp.dot(
                lhs, upper[: (h + 1) * span, cols], preferred_element_type=jnp.float32
            ).reshape(slices, tall, span)
        for g in range(group):
            sub = slice(g * band, (g + 1) * band)
            at = pl.ds(pl.multiple_of((step * group + g) * band, band), band)
            outs = []
            for j in range(cells // LANES):
                cols = slice(j * LANES, (j + 1) * LANES)
                before = jnp.zeros((band, LANES), jnp.float32)
                through = jnp.ones((band, LANES), jnp.float32)
                base = jnp.zeros((band, LANES), jnp.float32)
                lit = jnp.zeros((band, LANES), jnp.float32)
                for z in range(slices):
                    clipped = masked[z, sub, cols].astype(jnp.float32)
                    before = before + clipped
                    behind = jnp.exp2(before * depth_scale)
                    emitted = clipped * (through - behind)
                    through = behind
                    shade = inside[z, sub, cols]
                    if has_nearer:
                        shade = shade + nearer_ref[z, at, :]
                    base = base + emitted
                    lit = lit + emitted * jnp.exp2(shade * light_scale)
                outs.append((base, lit, before))
            for channel in range(3):
                for pair in range(shares // 2):
                    halves = []
                    for side in range(2):
                        first = (2 * pair + side) * share_rows
                        halves.append(jnp.concatenate([o[channel][first : first + share_rows] for o in outs], axis=0))
                    to = (step * group + g) * (shares // 2) + pair
                    keep_ref[channel, to] = jnp.where(odd, halves[1], halves[0])
                    give_ref[channel, to] = jnp.where(odd, halves[0], halves[1])
        return carry

    lax.fori_loop(0, rows // tall, work, 0)


def composite_slab(clip_flags, density, nearer, kappa, extinct, depth_n):
    slices, rows, cells = density.shape
    share_rows = rows // depth_n
    blocks_r, blocks_x = clip_flags.shape[1:]
    half = (3, depth_n // 2, share_rows * cells // LANES, LANES)
    log2e = math.log2(math.e)
    has_nearer = nearer is not None
    tall = math.gcd(blocks_r, 2) * rows // blocks_r
    vmem = pl.BlockSpec(memory_space=pltpu.VMEM)
    return pl.pallas_call(
        functools.partial(slab_kernel, -kappa * log2e, -extinct * log2e, share_rows, has_nearer),
        out_shape=[pltpu.VMEM(half, jnp.float32)] * 2,
        in_specs=[pl.BlockSpec(memory_space=pltpu.HBM)] * 2 + [vmem] * has_nearer,
        out_specs=[vmem, vmem],
        scratch_shapes=[
            pltpu.VMEM((slices, rows, cells), jnp.bfloat16),
            pltpu.VMEM((slices, tall, cells), jnp.bfloat16),
            pltpu.VMEM((slices, tall, cells), jnp.float32),
            pltpu.VMEM((cells, cells), jnp.bfloat16),
            pltpu.SMEM((blocks_r, blocks_x, slices), jnp.int32),
            pltpu.SemaphoreType.DMA((rows // tall,)),
            pltpu.SemaphoreType.DMA,
        ],
        compiler_params=pltpu.CompilerParams(vmem_limit_bytes=24 * 2**20),
        cost_estimate=pl.CostEstimate(
            flops=2 * slices * rows * cells * cells,
            bytes_accessed=2 * slices * rows * cells,
            transcendentals=2 * slices * rows * cells,
        ),
        name="slab",
    )(
        pltpu.with_memory_space_constraint(clip_flags.transpose(1, 2, 0), pltpu.HBM),
        pltpu.with_memory_space_constraint(density, pltpu.HBM),
        *([nearer] if has_nearer else []),
    )


def step_of(position, hop, count, ring):
    if ring:
        turn = ((position & 1) << 1 | position >> 1) + hop & 3
        return (turn & 1) << 1 | turn >> 1
    return position ^ hop


def sending_order(count, ring):
    if count < 4:
        return (1,)
    return (1, 3, 2) if ring else (3, 2, 1)


def sent_and_held(pieces, low, ring):
    depth_n = lax.axis_size("depth")
    count = len(pieces)
    held = []
    for hop in sending_order(count, ring):
        pairs = []
        for source in range(depth_n):
            position = source >> low & (count - 1)
            pairs.append((source, source + ((step_of(position, hop, count, ring) - position) << low)))
        held.append(lax.ppermute(pieces[hop], "depth", pairs))
    return [*held, pieces[0]]


def over(kappa, places, held):
    base, lit, column = 0.0, 0.0, 0.0
    for place, piece in zip(places, held):
        ahead = 0.0
        for other, front in zip(places, held):
            if front is not piece:
                ahead = ahead + jnp.where(other < place, front[2], 0.0)
        passed = jnp.exp(-kappa * ahead)
        base = base + piece[0] * passed
        lit = lit + piece[1] * passed
        column = column + piece[2]
    return base, lit, column


def places_of(order_ref, low, count, ring):
    mine = lax.axis_index("depth") >> low & (count - 1)
    flips = order_ref[0:1, 0:1] >> low & (count - 1)
    return [flips ^ step_of(mine, -hop if ring else hop, count, ring) for hop in (*sending_order(count, ring), 0)]


def merge_kernel(kappa, low, count, ring, next_ring, order_ref, *refs):
    held, out = refs[:count], refs[count:]
    places = places_of(order_ref, low, count, ring)
    fan = len(out)
    mine = lax.axis_index("depth") >> (low + count.bit_length() - 1) & (fan - 1)
    for hop in range(fan):
        for row in range(out[hop].shape[1]):
            at = row * fan + step_of(mine, hop, fan, next_ring)
            merged = over(kappa, places, [[piece[channel, at] for channel in range(3)] for piece in held])
            for channel in range(3):
                out[hop][channel, row] = merged[channel]


def opacity(depth):
    series = 1.0 - depth * (1.0 / 6.0)
    for term in (5.0, 4.0, 3.0, 2.0):
        series = 1.0 - depth * (1.0 / term) * series
    return jnp.where(depth < 0.125, depth * series, 1.0 - jnp.exp(-depth))


def glow_kernel(share_rows, offset_ref, ambient_ref, diffuse_ref, glow_ref):
    shape = glow_ref.shape[2:]
    row = lax.broadcasted_iota(jnp.int32, shape, 0) % share_rows + lax.axis_index("depth") * share_rows
    row = (row + offset_ref[0:1, 0:1]).astype(jnp.float32)
    source = 0.6 + 0.4 * jnp.cos(2.0 * math.pi * row / 64.0)
    for channel in range(3):
        glow_ref[0, channel] = jnp.broadcast_to(ambient_ref[0:1, channel : channel + 1], shape)
        glow_ref[1, channel] = diffuse_ref[0:1, channel : channel + 1] * source


def finish_kernel(kappa, low, count, ring, order_ref, glow_ref, *refs):
    held, image = refs[:count], refs[count]
    places = places_of(order_ref, low, count, ring)
    base, lit, column = over(kappa, places, [[piece[channel, 0] for channel in range(3)] for piece in held])
    share_rows = image.shape[1]
    for channel in range(4):
        if channel < 3:
            value = glow_ref[0, channel] * base + glow_ref[1, channel] * lit
        else:
            value = opacity(kappa * column)
        for j in range(image.shape[2] // LANES):
            image[channel, :, j * LANES : (j + 1) * LANES] = value[j * share_rows : (j + 1) * share_rows]


def on_device(density, clip_flags, band_offset, order, ambient, diffuse):
    slices, rows, cells = density.shape
    depth_n = lax.axis_size("depth")
    xs_n = lax.axis_size("xs")
    kappa = 2.0 / (slices * depth_n)
    extinct = 2.0 / (cells * xs_n)
    share_rows = rows // depth_n
    levels = depth_n.bit_length() - 1
    my_slab = lax.axis_index("depth")
    nearer = None
    if xs_n > 1:
        blocks_r, blocks_x = clip_flags.shape[1:]
        kept = density.astype(jnp.float32).reshape(
            slices, blocks_r, rows // blocks_r, blocks_x, cells // blocks_x
        )
        totals = jnp.sum(kept, axis=4) * clip_flags[:, :, None, :].astype(jnp.float32)
        totals = jnp.sum(totals, axis=3).reshape(slices, rows)
        nearer = prefix(totals, "xs", lambda early, late: early + late, jnp.zeros_like(totals))
        nearer = nearer[:, :, None]
    held = sent_and_held(composite_slab(clip_flags, density, nearer, kappa, extinct, depth_n), 0, False)
    first = order[None]
    vmem = pl.BlockSpec(memory_space=pltpu.VMEM)
    low, ring = 0, False
    while True:
        count = len(held)
        through = low + count.bit_length() - 1
        if through == levels:
            break
        fan = 4 if through + 1 < levels else 2
        next_ring = low > 0 and fan == 4
        shape = (3, held[0].shape[1] // fan, *held[0].shape[2:])
        pieces = pl.pallas_call(
            functools.partial(merge_kernel, kappa, low, count, ring, next_ring),
            out_shape=[pltpu.VMEM(shape, jnp.float32)] * fan,
            in_specs=[vmem] * (1 + count),
            out_specs=[vmem] * fan,
            compiler_params=pltpu.CompilerParams(vmem_limit_bytes=4 * 2**20),
            name="merge",
        )(first, *held)
        low, ring = through, next_ring
        held = sent_and_held(pieces, low, ring)
    glow = pl.pallas_call(
        functools.partial(glow_kernel, share_rows),
        out_shape=pltpu.VMEM((2, 3, share_rows * cells // LANES, LANES), jnp.float32),
        in_specs=[vmem] * 3,
        out_specs=vmem,
        compiler_params=pltpu.CompilerParams(vmem_limit_bytes=4 * 2**20),
        cost_estimate=pl.CostEstimate(flops=10**5, bytes_accessed=10**5, transcendentals=2048),
        name="glow",
    )(band_offset[None], ambient[None], diffuse[None])
    return pl.pallas_call(
        functools.partial(finish_kernel, kappa, low, len(held), ring),
        out_shape=jax.ShapeDtypeStruct((4, share_rows, cells), jnp.float32),
        in_specs=[vmem] * (2 + len(held)),
        compiler_params=pltpu.CompilerParams(vmem_limit_bytes=4 * 2**20),
        name="finish",
    )(first, glow, *held)


def solution(mesh):
    return jax.shard_map(
        on_device,
        mesh=mesh,
        in_specs=(P("depth", None, "xs"), P("depth", None, "xs"), P(), P(), P(), P()),
        out_specs=P(None, "depth", "xs"),
        check_vma=False,
    )
```

```python
import functools
import math

import jax
import jax.numpy as jnp
from jax import lax
from jax.experimental import pallas as pl
from jax.experimental.pallas import tpu as pltpu

from jax.sharding import PartitionSpec as P

LANES = 128

def prefix(value, axis, join, neutral):
    count, mine = (lax.axis_size(axis), lax.axis_index(axis))
    pieces = lax.all_gather(value, axis)
    so_far = jnp.full_like(value, 0) + jnp.asarray(neutral, value.dtype)

    def lap(position, so_far):
        longer = join(so_far, pieces[position])
        return jnp.where(position < mine, longer, so_far)

    return lax.fori_loop(0, count - 1, lap, so_far)


def slab_kernel(depth_scale, light_scale, share_rows, has_nearer, flags_hbm, dens_ref, *rest):
    if has_nearer:
        nearer_ref, *rest = rest
    keep_ref, give_ref, dens, masked, inside, upper, flags, sems, flag_sem = rest
    slices, rows, cells = dens.shape
    blocks_r, blocks_x = flags.shape[:2]
    band = rows // blocks_r
    width = cells // blocks_x
    span = math.gcd(cells, 2 * LANES)
    group = masked.shape[1] // band
    tall = group * band
    shares = band // share_rows

    def copy(step):
        at = pl.ds(pl.multiple_of(step * tall, tall), tall)
        return pltpu.make_async_copy(dens_ref.at[:, at, :], dens.at[:, at, :], sems.at[step])

    flag_copy = pltpu.make_async_copy(flags_hbm, flags, flag_sem)
    flag_copy.start()
    for step in range(rows // tall):
        copy(step).start()
    upper[...] = (
        lax.broadcasted_iota(jnp.int32, (cells, cells), 0) < lax.broadcasted_iota(jnp.int32, (cells, cells), 1)
    ).astype(jnp.float32).astype(jnp.bfloat16)
    me = lax.axis_index("depth")
    odd = me & 1 == 1
    fan = give_ref.shape[0]
    mine = me >> 1 & (fan - 1)
    laps = group * (shares // 2) // fan
    flag_copy.wait()

    def work(step, carry):
        copy(step).wait()
        for g in range(group):
            block = step * group + g
            at = pl.ds(pl.multiple_of(block * band, band), band)
            for j in range(blocks_x):
                for z in range(slices):
                    flag = flags[block, j, z].astype(jnp.float32)
                    flag = jnp.full((band, width), flag, jnp.float32).astype(jnp.bfloat16)
                    cols = slice(j * width, (j + 1) * width)
                    masked[z, g * band : (g + 1) * band, cols] = dens[z, at, cols] * flag
        for h in range(cells // span):
            lhs = masked[:, :, : (h + 1) * span].reshape(slices * tall, (h + 1) * span)
            cols = slice(h * span, (h + 1) * span)
            inside[:, :, cols] = jnp.dot(
                lhs, upper[: (h + 1) * span, cols], preferred_element_type=jnp.float32
            ).reshape(slices, tall, span)
        for g in range(group):
            sub = slice(g * band, (g + 1) * band)
            at = pl.ds(pl.multiple_of((step * group + g) * band, band), band)
            outs = []
            for j in range(cells // LANES):
                cols = slice(j * LANES, (j + 1) * LANES)
                before = jnp.zeros((band, LANES), jnp.float32)
                through = jnp.ones((band, LANES), jnp.float32)
                base = jnp.zeros((band, LANES), jnp.float32)
                lit = jnp.zeros((band, LANES), jnp.float32)
                for z in range(slices):
                    clipped = masked[z, sub, cols].astype(jnp.float32)
                    before = before + clipped
                    behind = jnp.exp2(before * depth_scale)
                    emitted = clipped * (through - behind)
                    through = behind
                    shade = inside[z, sub, cols]
                    if has_nearer:
                        shade = shade + nearer_ref[z, at, :]
                    base = base + emitted
                    lit = lit + emitted * jnp.exp2(shade * light_scale)
                outs.append((base, lit, before))
            for channel in range(3):
                for pair in range(shares // 2):
                    halves = []
                    for side in range(2):
                        first = (2 * pair + side) * share_rows
                        halves.append(jnp.concatenate([o[channel][first : first + share_rows] for o in outs], axis=0))
                    local = g * (shares // 2) + pair
                    hop, row = mine ^ local % fan, step * laps + local // fan
                    keep_ref[hop, channel, row] = jnp.where(odd, halves[1], halves[0])
                    give_ref[hop, channel, row] = jnp.where(odd, halves[0], halves[1])
        return carry

    lax.fori_loop(0, rows // tall, work, 0)


def composite_slab(clip_flags, density, nearer, kappa, extinct, depth_n, fan):
    slices, rows, cells = density.shape
    share_rows = rows // depth_n
    blocks_r, blocks_x = clip_flags.shape[1:]
    half = (fan, 3, depth_n // 2 // fan, share_rows * cells // LANES, LANES)
    log2e = math.log2(math.e)
    has_nearer = nearer is not None
    tall = math.gcd(blocks_r, 2) * rows // blocks_r
    vmem = pl.BlockSpec(memory_space=pltpu.VMEM)
    return pl.pallas_call(
        functools.partial(slab_kernel, -kappa * log2e, -extinct * log2e, share_rows, has_nearer),
        out_shape=[pltpu.VMEM(half, jnp.float32)] * 2,
        in_specs=[pl.BlockSpec(memory_space=pltpu.HBM)] * 2 + [vmem] * has_nearer,
        out_specs=[vmem, vmem],
        scratch_shapes=[
            pltpu.VMEM((slices, rows, cells), jnp.bfloat16),
            pltpu.VMEM((slices, tall, cells), jnp.bfloat16),
            pltpu.VMEM((slices, tall, cells), jnp.float32),
            pltpu.VMEM((cells, cells), jnp.bfloat16),
            pltpu.SMEM((blocks_r, blocks_x, slices), jnp.int32),
            pltpu.SemaphoreType.DMA((rows // tall,)),
            pltpu.SemaphoreType.DMA,
        ],
        compiler_params=pltpu.CompilerParams(vmem_limit_bytes=24 * 2**20),
        cost_estimate=pl.CostEstimate(
            flops=2 * slices * rows * cells * cells,
            bytes_accessed=2 * slices * rows * cells,
            transcendentals=2 * slices * rows * cells,
        ),
        name="slab",
    )(
        pltpu.with_memory_space_constraint(clip_flags.transpose(1, 2, 0), pltpu.HBM),
        pltpu.with_memory_space_constraint(density, pltpu.HBM),
        *([nearer] if has_nearer else []),
    )


def step_of(position, hop, count, ring):
    if ring:
        turn = ((position & 1) << 1 | position >> 1) + hop & 3
        return (turn & 1) << 1 | turn >> 1
    return position ^ hop


def sending_order(count, ring):
    if count < 4:
        return (1,)
    return (1, 3, 2) if ring else (3, 2, 1)


def sent_and_held(pieces, low, ring):
    depth_n = lax.axis_size("depth")
    count = len(pieces)
    held = []
    for hop in sending_order(count, ring):
        pairs = []
        for source in range(depth_n):
            position = source >> low & (count - 1)
            pairs.append((source, source + ((step_of(position, hop, count, ring) - position) << low)))
        held.append(lax.ppermute(pieces[hop], "depth", pairs))
    return [*held, pieces[0]]


def over(kappa, places, held):
    base, lit, column = 0.0, 0.0, 0.0
    for place, piece in zip(places, held):
        ahead = 0.0
        for other, front in zip(places, held):
            if front is not piece:
                ahead = ahead + jnp.where(other < place, front[2], 0.0)
        passed = jnp.exp(-kappa * ahead)
        base = base + piece[0] * passed
        lit = lit + piece[1] * passed
        column = column + piece[2]
    return base, lit, column


def places_of(order_ref, low, count, ring):
    mine = lax.axis_index("depth") >> low & (count - 1)
    flips = order_ref[0:1, 0:1] >> low & (count - 1)
    return [flips ^ step_of(mine, -hop if ring else hop, count, ring) for hop in (*sending_order(count, ring), 0)]


def merge_kernel(kappa, low, count, ring, next_ring, order_ref, *refs):
    held, out = refs[:count], refs[count:]
    places = places_of(order_ref, low, count, ring)
    fan = len(out)
    mine = lax.axis_index("depth") >> (low + count.bit_length() - 1) & (fan - 1)
    for hop in range(fan):
        for row in range(out[hop].shape[1]):
            at = row * fan + step_of(mine, hop, fan, next_ring)
            merged = over(kappa, places, [[piece[channel, at] for channel in range(3)] for piece in held])
            for channel in range(3):
                out[hop][channel, row] = merged[channel]


def pair_kernel(kappa, first, order_ref, keep_ref, recv_ref, *out):
    places = places_of(order_ref, 0, 2, False)
    for at, piece in enumerate(out):
        for row in range(piece.shape[1]):
            held = [[recv_ref[at, channel, row] for channel in range(3)], [keep_ref[first + at, channel, row] for channel in range(3)]]
            merged = over(kappa, places, held)
            for channel in range(3):
                piece[channel, row] = merged[channel]


def opacity(depth):
    series = 1.0 - depth * (1.0 / 6.0)
    for term in (5.0, 4.0, 3.0, 2.0):
        series = 1.0 - depth * (1.0 / term) * series
    return jnp.where(depth < 0.125, depth * series, 1.0 - jnp.exp(-depth))


def glow_kernel(share_rows, offset_ref, ambient_ref, diffuse_ref, glow_ref):
    shape = glow_ref.shape[2:]
    row = lax.broadcasted_iota(jnp.int32, shape, 0) % share_rows + lax.axis_index("depth") * share_rows
    row = (row + offset_ref[0:1, 0:1]).astype(jnp.float32)
    source = 0.6 + 0.4 * jnp.cos(2.0 * math.pi * row / 64.0)
    for channel in range(3):
        glow_ref[0, channel] = jnp.broadcast_to(ambient_ref[0:1, channel : channel + 1], shape)
        glow_ref[1, channel] = diffuse_ref[0:1, channel : channel + 1] * source


def finish_kernel(kappa, low, count, ring, order_ref, glow_ref, *refs):
    held, image = refs[:count], refs[count]
    places = places_of(order_ref, low, count, ring)
    base, lit, column = over(kappa, places, [[piece[channel, 0] for channel in range(3)] for piece in held])
    share_rows = image.shape[1]
    for channel in range(4):
        if channel < 3:
            value = glow_ref[0, channel] * base + glow_ref[1, channel] * lit
        else:
            value = opacity(kappa * column)
        for j in range(image.shape[2] // LANES):
            image[channel, :, j * LANES : (j + 1) * LANES] = value[j * share_rows : (j + 1) * share_rows]


def on_device(density, clip_flags, band_offset, order, ambient, diffuse):
    slices, rows, cells = density.shape
    depth_n = lax.axis_size("depth")
    xs_n = lax.axis_size("xs")
    kappa = 2.0 / (slices * depth_n)
    extinct = 2.0 / (cells * xs_n)
    share_rows = rows // depth_n
    levels = depth_n.bit_length() - 1
    my_slab = lax.axis_index("depth")
    nearer = None
    if xs_n > 1:
        blocks_r, blocks_x = clip_flags.shape[1:]
        kept = density.astype(jnp.float32).reshape(
            slices, blocks_r, rows // blocks_r, blocks_x, cells // blocks_x
        )
        totals = jnp.sum(kept, axis=4) * clip_flags[:, :, None, :].astype(jnp.float32)
        totals = jnp.sum(totals, axis=3).reshape(slices, rows)
        nearer = prefix(totals, "xs", lambda early, late: early + late, jnp.zeros_like(totals))
        nearer = nearer[:, :, None]
    first = order[None]
    vmem = pl.BlockSpec(memory_space=pltpu.VMEM)
    small = pltpu.CompilerParams(vmem_limit_bytes=4 * 2**20)
    fan = 4
    keep, give = composite_slab(clip_flags, density, nearer, kappa, extinct, depth_n, fan)
    pairs = [(source, source ^ 1) for source in range(depth_n)]
    far = lax.ppermute(give[fan - 1 :], "depth", pairs)
    near = lax.ppermute(give[: fan - 1], "depth", pairs)

    def paired(start, recv):
        return pl.pallas_call(
            functools.partial(pair_kernel, kappa, start),
            out_shape=[pltpu.VMEM(keep.shape[1:], jnp.float32)] * recv.shape[0],
            in_specs=[vmem] * 3,
            out_specs=[vmem] * recv.shape[0],
            compiler_params=small,
            name="pair",
        )(first, keep, recv)

    farthest = paired(fan - 1, far)
    pieces = [*paired(0, near), *farthest]
    low, ring = 1, False
    held = sent_and_held(pieces, low, ring)
    while True:
        count = len(held)
        through = low + count.bit_length() - 1
        if through == levels:
            break
        fan = 4 if through + 1 < levels else 2
        next_ring = fan == 4
        shape = (3, held[0].shape[1] // fan, *held[0].shape[2:])
        pieces = pl.pallas_call(
            functools.partial(merge_kernel, kappa, low, count, ring, next_ring),
            out_shape=[pltpu.VMEM(shape, jnp.float32)] * fan,
            in_specs=[vmem] * (1 + count),
            out_specs=[vmem] * fan,
            compiler_params=small,
            name="merge",
        )(first, *held)
        low, ring = through, next_ring
        held = sent_and_held(pieces, low, ring)
    glow = pl.pallas_call(
        functools.partial(glow_kernel, share_rows),
        out_shape=pltpu.VMEM((2, 3, share_rows * cells // LANES, LANES), jnp.float32),
        in_specs=[vmem] * 3,
        out_specs=vmem,
        compiler_params=small,
        cost_estimate=pl.CostEstimate(flops=10**5, bytes_accessed=10**5, transcendentals=2048),
        name="glow",
    )(band_offset[None], ambient[None], diffuse[None])
    return pl.pallas_call(
        functools.partial(finish_kernel, kappa, low, len(held), ring),
        out_shape=jax.ShapeDtypeStruct((4, share_rows, cells), jnp.float32),
        in_specs=[vmem] * (2 + len(held)),
        compiler_params=small,
        name="finish",
    )(first, glow, *held)


def solution(mesh):
    return jax.shard_map(
        on_device,
        mesh=mesh,
        in_specs=(P("depth", None, "xs"), P("depth", None, "xs"), P(), P(), P(), P()),
        out_specs=P(None, "depth", "xs"),
        check_vma=False,
    )
```

```python
import functools
import math

import jax
import jax.numpy as jnp
from jax import lax
from jax.experimental import pallas as pl
from jax.experimental.pallas import tpu as pltpu

from jax.sharding import PartitionSpec as P

LANES = 128

def prefix(value, axis, join, neutral):
    count, mine = (lax.axis_size(axis), lax.axis_index(axis))
    pieces = lax.all_gather(value, axis)
    so_far = jnp.full_like(value, 0) + jnp.asarray(neutral, value.dtype)

    def lap(position, so_far):
        longer = join(so_far, pieces[position])
        return jnp.where(position < mine, longer, so_far)

    return lax.fori_loop(0, count - 1, lap, so_far)


def slab_kernel(depth_scale, light_scale, share_rows, has_nearer, flags_hbm, dens_ref, *rest):
    if has_nearer:
        nearer_ref, *rest = rest
    keep_ref, give_ref, dens, masked, inside, upper, flags, sems, flag_sem = rest
    slices, rows, cells = dens.shape
    blocks_r, blocks_x = flags.shape[:2]
    band = rows // blocks_r
    width = cells // blocks_x
    span = math.gcd(cells, 2 * LANES)
    group = masked.shape[1] // band
    tall = group * band
    shares = band // share_rows

    def copy(step):
        at = pl.ds(pl.multiple_of(step * tall, tall), tall)
        return pltpu.make_async_copy(dens_ref.at[:, at, :], dens.at[:, at, :], sems.at[step])

    flag_copy = pltpu.make_async_copy(flags_hbm, flags, flag_sem)
    flag_copy.start()
    for step in range(rows // tall):
        copy(step).start()
    upper[...] = (
        lax.broadcasted_iota(jnp.int32, (cells, cells), 0) < lax.broadcasted_iota(jnp.int32, (cells, cells), 1)
    ).astype(jnp.float32).astype(jnp.bfloat16)
    odd = lax.axis_index("depth") & 1 == 1
    flag_copy.wait()

    def work(step, carry):
        copy(step).wait()
        for g in range(group):
            block = step * group + g
            at = pl.ds(pl.multiple_of(block * band, band), band)
            for j in range(blocks_x):
                for z in range(slices):
                    flag = flags[block, j, z].astype(jnp.float32)
                    flag = jnp.full((band, width), flag, jnp.float32).astype(jnp.bfloat16)
                    cols = slice(j * width, (j + 1) * width)
                    masked[z, g * band : (g + 1) * band, cols] = dens[z, at, cols] * flag
        for h in range(cells // span):
            lhs = masked[:, :, : (h + 1) * span].reshape(slices * tall, (h + 1) * span)
            cols = slice(h * span, (h + 1) * span)
            inside[:, :, cols] = jnp.dot(
                lhs, upper[: (h + 1) * span, cols], preferred_element_type=jnp.float32
            ).reshape(slices, tall, span)
        for g in range(group):
            sub = slice(g * band, (g + 1) * band)
            at = pl.ds(pl.multiple_of((step * group + g) * band, band), band)
            outs = []
            for j in range(cells // LANES):
                cols = slice(j * LANES, (j + 1) * LANES)
                before = jnp.zeros((band, LANES), jnp.float32)
                through = jnp.ones((band, LANES), jnp.float32)
                base = jnp.zeros((band, LANES), jnp.float32)
                lit = jnp.zeros((band, LANES), jnp.float32)
                for z in range(slices):
                    clipped = masked[z, sub, cols].astype(jnp.float32)
                    before = before + clipped
                    behind = jnp.exp2(before * depth_scale)
                    emitted = clipped * (through - behind)
                    through = behind
                    shade = inside[z, sub, cols]
                    if has_nearer:
                        shade = shade + nearer_ref[z, at, :]
                    base = base + emitted
                    lit = lit + emitted * jnp.exp2(shade * light_scale)
                outs.append((base, lit, before))
            for channel in range(3):
                for pair in range(shares // 2):
                    halves = []
                    for side in range(2):
                        first = (2 * pair + side) * share_rows
                        halves.append(jnp.concatenate([o[channel][first : first + share_rows] for o in outs], axis=0))
                    to = (step * group + g) * (shares // 2) + pair
                    keep_ref[channel, to] = jnp.where(odd, halves[1], halves[0])
                    give_ref[channel, to] = jnp.where(odd, halves[0], halves[1])
        return carry

    lax.fori_loop(0, rows // tall, work, 0)


def composite_slab(clip_flags, density, nearer, kappa, extinct, depth_n):
    slices, rows, cells = density.shape
    share_rows = rows // depth_n
    blocks_r, blocks_x = clip_flags.shape[1:]
    half = (3, depth_n // 2, share_rows * cells // LANES, LANES)
    log2e = math.log2(math.e)
    has_nearer = nearer is not None
    tall = math.gcd(blocks_r, 2) * rows // blocks_r
    vmem = pl.BlockSpec(memory_space=pltpu.VMEM)
    return pl.pallas_call(
        functools.partial(slab_kernel, -kappa * log2e, -extinct * log2e, share_rows, has_nearer),
        out_shape=[pltpu.VMEM(half, jnp.float32)] * 2,
        in_specs=[pl.BlockSpec(memory_space=pltpu.HBM)] * 2 + [vmem] * has_nearer,
        out_specs=[vmem, vmem],
        scratch_shapes=[
            pltpu.VMEM((slices, rows, cells), jnp.bfloat16),
            pltpu.VMEM((slices, tall, cells), jnp.bfloat16),
            pltpu.VMEM((slices, tall, cells), jnp.float32),
            pltpu.VMEM((cells, cells), jnp.bfloat16),
            pltpu.SMEM((blocks_r, blocks_x, slices), jnp.int32),
            pltpu.SemaphoreType.DMA((rows // tall,)),
            pltpu.SemaphoreType.DMA,
        ],
        compiler_params=pltpu.CompilerParams(vmem_limit_bytes=24 * 2**20),
        cost_estimate=pl.CostEstimate(
            flops=2 * slices * rows * cells * cells,
            bytes_accessed=2 * slices * rows * cells,
            transcendentals=2 * slices * rows * cells,
        ),
        name="slab",
    )(
        pltpu.with_memory_space_constraint(clip_flags.transpose(1, 2, 0), pltpu.HBM),
        pltpu.with_memory_space_constraint(density, pltpu.HBM),
        *([nearer] if has_nearer else []),
    )


def step_of(position, hop, count, ring):
    if ring == 1:
        turn = (position ^ position >> 1) + hop & 3
        return turn ^ turn >> 1
    if ring == 2:
        turn = ((position & 1) << 1 | position >> 1) + hop & 3
        return (turn & 1) << 1 | turn >> 1
    return position ^ hop


def sending_order(count, ring):
    if count < 4:
        return (1,)
    return (2, 1, 3) if ring == 1 else (1, 3, 2)


def sent_and_held(pieces, low, ring):
    depth_n = lax.axis_size("depth")
    count = len(pieces)
    held = []
    for hop in sending_order(count, ring):
        pairs = []
        for source in range(depth_n):
            position = source >> low & (count - 1)
            pairs.append((source, source + ((step_of(position, hop, count, ring) - position) << low)))
        held.append(lax.ppermute(pieces[hop], "depth", pairs))
    return [*held, pieces[0]]


def over(kappa, places, held):
    base, lit, column = 0.0, 0.0, 0.0
    for place, piece in zip(places, held):
        ahead = 0.0
        for other, front in zip(places, held):
            if front is not piece:
                ahead = ahead + jnp.where(other < place, front[2], 0.0)
        passed = jnp.exp(-kappa * ahead)
        base = base + piece[0] * passed
        lit = lit + piece[1] * passed
        column = column + piece[2]
    return base, lit, column


def places_of(order_ref, low, count, ring):
    mine = lax.axis_index("depth") >> low & (count - 1)
    flips = order_ref[0:1, 0:1] >> low & (count - 1)
    return [flips ^ step_of(mine, -hop if ring else hop, count, ring) for hop in (*sending_order(count, ring), 0)]


def merge_kernel(kappa, low, count, ring, next_ring, order_ref, *refs):
    held, out = refs[:count], refs[count:]
    places = places_of(order_ref, low, count, ring)
    fan = len(out)
    mine = lax.axis_index("depth") >> (low + count.bit_length() - 1) & (fan - 1)
    for hop in range(fan):
        for row in range(out[hop].shape[1]):
            at = row * fan + step_of(mine, hop, fan, next_ring)
            merged = over(kappa, places, [[piece[channel, at] for channel in range(3)] for piece in held])
            for channel in range(3):
                out[hop][channel, row] = merged[channel]


def opacity(depth):
    series = 1.0 - depth * (1.0 / 6.0)
    for term in (5.0, 4.0, 3.0, 2.0):
        series = 1.0 - depth * (1.0 / term) * series
    return jnp.where(depth < 0.125, depth * series, 1.0 - jnp.exp(-depth))


def glow_kernel(share_rows, offset_ref, ambient_ref, diffuse_ref, glow_ref):
    shape = glow_ref.shape[2:]
    row = lax.broadcasted_iota(jnp.int32, shape, 0) % share_rows + lax.axis_index("depth") * share_rows
    row = (row + offset_ref[0:1, 0:1]).astype(jnp.float32)
    source = 0.6 + 0.4 * jnp.cos(2.0 * math.pi * row / 64.0)
    for channel in range(3):
        glow_ref[0, channel] = jnp.broadcast_to(ambient_ref[0:1, channel : channel + 1], shape)
        glow_ref[1, channel] = diffuse_ref[0:1, channel : channel + 1] * source


def finish_kernel(kappa, low, count, ring, order_ref, glow_ref, *refs):
    held, image = refs[:count], refs[count]
    places = places_of(order_ref, low, count, ring)
    base, lit, column = over(kappa, places, [[piece[channel, 0] for channel in range(3)] for piece in held])
    share_rows = image.shape[1]
    for channel in range(4):
        if channel < 3:
            value = glow_ref[0, channel] * base + glow_ref[1, channel] * lit
        else:
            value = opacity(kappa * column)
        for j in range(image.shape[2] // LANES):
            image[channel, :, j * LANES : (j + 1) * LANES] = value[j * share_rows : (j + 1) * share_rows]


def on_device(density, clip_flags, band_offset, order, ambient, diffuse):
    slices, rows, cells = density.shape
    depth_n = lax.axis_size("depth")
    xs_n = lax.axis_size("xs")
    kappa = 2.0 / (slices * depth_n)
    extinct = 2.0 / (cells * xs_n)
    share_rows = rows // depth_n
    levels = depth_n.bit_length() - 1
    my_slab = lax.axis_index("depth")
    nearer = None
    if xs_n > 1:
        blocks_r, blocks_x = clip_flags.shape[1:]
        kept = density.astype(jnp.float32).reshape(
            slices, blocks_r, rows // blocks_r, blocks_x, cells // blocks_x
        )
        totals = jnp.sum(kept, axis=4) * clip_flags[:, :, None, :].astype(jnp.float32)
        totals = jnp.sum(totals, axis=3).reshape(slices, rows)
        nearer = prefix(totals, "xs", lambda early, late: early + late, jnp.zeros_like(totals))
        nearer = nearer[:, :, None]
    held = sent_and_held(composite_slab(clip_flags, density, nearer, kappa, extinct, depth_n), 0, 0)
    first = order[None]
    vmem = pl.BlockSpec(memory_space=pltpu.VMEM)
    low, ring = 0, 0
    while True:
        count = len(held)
        through = low + count.bit_length() - 1
        if through == levels:
            break
        fan = 4 if through + 1 < levels else 2
        next_ring = 0 if fan < 4 else 1 if low == 0 else 2
        shape = (3, held[0].shape[1] // fan, *held[0].shape[2:])
        pieces = pl.pallas_call(
            functools.partial(merge_kernel, kappa, low, count, ring, next_ring),
            out_shape=[pltpu.VMEM(shape, jnp.float32)] * fan,
            in_specs=[vmem] * (1 + count),
            out_specs=[vmem] * fan,
            compiler_params=pltpu.CompilerParams(vmem_limit_bytes=4 * 2**20),
            name="merge",
        )(first, *held)
        low, ring = through, next_ring
        held = sent_and_held(pieces, low, ring)
    glow = pl.pallas_call(
        functools.partial(glow_kernel, share_rows),
        out_shape=pltpu.VMEM((2, 3, share_rows * cells // LANES, LANES), jnp.float32),
        in_specs=[vmem] * 3,
        out_specs=vmem,
        compiler_params=pltpu.CompilerParams(vmem_limit_bytes=4 * 2**20),
        cost_estimate=pl.CostEstimate(flops=10**5, bytes_accessed=10**5, transcendentals=2048),
        name="glow",
    )(band_offset[None], ambient[None], diffuse[None])
    return pl.pallas_call(
        functools.partial(finish_kernel, kappa, low, len(held), ring),
        out_shape=jax.ShapeDtypeStruct((4, share_rows, cells), jnp.float32),
        in_specs=[vmem] * (2 + len(held)),
        compiler_params=pltpu.CompilerParams(vmem_limit_bytes=4 * 2**20),
        name="finish",
    )(first, glow, *held)


def solution(mesh):
    return jax.shard_map(
        on_device,
        mesh=mesh,
        in_specs=(P("depth", None, "xs"), P("depth", None, "xs"), P(), P(), P(), P()),
        out_specs=P(None, "depth", "xs"),
        check_vma=False,
    )
```

```python
import functools
import math

import jax
import jax.numpy as jnp
from jax import lax
from jax.experimental import pallas as pl
from jax.experimental.pallas import tpu as pltpu

from jax.sharding import PartitionSpec as P

LANES = 128

def prefix(value, axis, join, neutral):
    count, mine = (lax.axis_size(axis), lax.axis_index(axis))
    pieces = lax.all_gather(value, axis)
    so_far = jnp.full_like(value, 0) + jnp.asarray(neutral, value.dtype)

    def lap(position, so_far):
        longer = join(so_far, pieces[position])
        return jnp.where(position < mine, longer, so_far)

    return lax.fori_loop(0, count - 1, lap, so_far)


def slab_kernel(depth_scale, light_scale, share_rows, has_nearer, flags_hbm, dens_ref, *rest):
    if has_nearer:
        nearer_ref, *rest = rest
    keep_ref, give_ref, dens, masked, inside, upper, flags, sems, flag_sem = rest
    slices, rows, cells = dens.shape
    blocks_r, blocks_x = flags.shape[:2]
    band = rows // blocks_r
    width = cells // blocks_x
    span = math.gcd(cells, 2 * LANES)
    group = masked.shape[1] // band
    tall = group * band
    shares = band // share_rows

    def copy(part):
        at = pl.ds(0, tall) if part == 0 else pl.ds(tall, rows - tall)
        return pltpu.make_async_copy(dens_ref.at[:, at, :], dens.at[:, at, :], sems.at[part])

    flag_copy = pltpu.make_async_copy(flags_hbm, flags, flag_sem)
    flag_copy.start()
    copy(0).start()
    copy(1).start()
    upper[...] = (
        lax.broadcasted_iota(jnp.int32, (cells, cells), 0) < lax.broadcasted_iota(jnp.int32, (cells, cells), 1)
    ).astype(jnp.float32).astype(jnp.bfloat16)
    odd = lax.axis_index("depth") & 1 == 1
    flag_copy.wait()

    def work(step, carry):
        @pl.when(step == 0)
        def _():
            copy(0).wait()

        @pl.when(step == 1)
        def _():
            copy(1).wait()

        for g in range(group):
            block = step * group + g
            at = pl.ds(pl.multiple_of(block * band, band), band)
            for j in range(blocks_x):
                for z in range(slices):
                    flag = flags[block, j, z].astype(jnp.float32)
                    flag = jnp.full((band, width), flag, jnp.float32).astype(jnp.bfloat16)
                    cols = slice(j * width, (j + 1) * width)
                    masked[z, g * band : (g + 1) * band, cols] = dens[z, at, cols] * flag
        for h in range(cells // span):
            lhs = masked[:, :, : (h + 1) * span].reshape(slices * tall, (h + 1) * span)
            cols = slice(h * span, (h + 1) * span)
            inside[:, :, cols] = jnp.dot(
                lhs, upper[: (h + 1) * span, cols], preferred_element_type=jnp.float32
            ).reshape(slices, tall, span)
        for g in range(group):
            sub = slice(g * band, (g + 1) * band)
            at = pl.ds(pl.multiple_of((step * group + g) * band, band), band)
            outs = []
            for j in range(cells // LANES):
                cols = slice(j * LANES, (j + 1) * LANES)
                before = jnp.zeros((band, LANES), jnp.float32)
                through = jnp.ones((band, LANES), jnp.float32)
                base = jnp.zeros((band, LANES), jnp.float32)
                lit = jnp.zeros((band, LANES), jnp.float32)
                for z in range(slices):
                    clipped = masked[z, sub, cols].astype(jnp.float32)
                    before = before + clipped
                    behind = jnp.exp2(before * depth_scale)
                    emitted = clipped * (through - behind)
                    through = behind
                    shade = inside[z, sub, cols]
                    if has_nearer:
                        shade = shade + nearer_ref[z, at, :]
                    base = base + emitted
                    lit = lit + emitted * jnp.exp2(shade * light_scale)
                outs.append((base, lit, before))
            for channel in range(3):
                for pair in range(shares // 2):
                    halves = []
                    for side in range(2):
                        first = (2 * pair + side) * share_rows
                        halves.append(jnp.concatenate([o[channel][first : first + share_rows] for o in outs], axis=0))
                    to = (step * group + g) * (shares // 2) + pair
                    keep_ref[channel, to] = jnp.where(odd, halves[1], halves[0])
                    give_ref[channel, to] = jnp.where(odd, halves[0], halves[1])
        return carry

    lax.fori_loop(0, rows // tall, work, 0)


def composite_slab(clip_flags, density, nearer, kappa, extinct, depth_n):
    slices, rows, cells = density.shape
    share_rows = rows // depth_n
    blocks_r, blocks_x = clip_flags.shape[1:]
    half = (3, depth_n // 2, share_rows * cells // LANES, LANES)
    log2e = math.log2(math.e)
    has_nearer = nearer is not None
    tall = math.gcd(blocks_r, 2) * rows // blocks_r
    vmem = pl.BlockSpec(memory_space=pltpu.VMEM)
    return pl.pallas_call(
        functools.partial(slab_kernel, -kappa * log2e, -extinct * log2e, share_rows, has_nearer),
        out_shape=[pltpu.VMEM(half, jnp.float32)] * 2,
        in_specs=[pl.BlockSpec(memory_space=pltpu.HBM)] * 2 + [vmem] * has_nearer,
        out_specs=[vmem, vmem],
        scratch_shapes=[
            pltpu.VMEM((slices, rows, cells), jnp.bfloat16),
            pltpu.VMEM((slices, tall, cells), jnp.bfloat16),
            pltpu.VMEM((slices, tall, cells), jnp.float32),
            pltpu.VMEM((cells, cells), jnp.bfloat16),
            pltpu.SMEM((blocks_r, blocks_x, slices), jnp.int32),
            pltpu.SemaphoreType.DMA((2,)),
            pltpu.SemaphoreType.DMA,
        ],
        compiler_params=pltpu.CompilerParams(vmem_limit_bytes=24 * 2**20),
        cost_estimate=pl.CostEstimate(
            flops=2 * slices * rows * cells * cells,
            bytes_accessed=2 * slices * rows * cells,
            transcendentals=2 * slices * rows * cells,
        ),
        name="slab",
    )(
        pltpu.with_memory_space_constraint(clip_flags.transpose(1, 2, 0), pltpu.HBM),
        pltpu.with_memory_space_constraint(density, pltpu.HBM),
        *([nearer] if has_nearer else []),
    )


def step_of(position, hop, count, ring):
    if ring:
        turn = ((position & 1) << 1 | position >> 1) + hop & 3
        return (turn & 1) << 1 | turn >> 1
    return position ^ hop


def sending_order(count, ring):
    if count < 4:
        return (1,)
    return (1, 3, 2) if ring else (3, 2, 1)


def sent_and_held(pieces, low, ring):
    depth_n = lax.axis_size("depth")
    count = len(pieces)
    held = []
    for hop in sending_order(count, ring):
        pairs = []
        for source in range(depth_n):
            position = source >> low & (count - 1)
            pairs.append((source, source + ((step_of(position, hop, count, ring) - position) << low)))
        held.append(lax.ppermute(pieces[hop], "depth", pairs))
    return [*held, pieces[0]]


def over(kappa, places, held):
    base, lit, column = 0.0, 0.0, 0.0
    for place, piece in zip(places, held):
        ahead = 0.0
        for other, front in zip(places, held):
            if front is not piece:
                ahead = ahead + jnp.where(other < place, front[2], 0.0)
        passed = jnp.exp(-kappa * ahead)
        base = base + piece[0] * passed
        lit = lit + piece[1] * passed
        column = column + piece[2]
    return base, lit, column


def places_of(order_ref, low, count, ring):
    mine = lax.axis_index("depth") >> low & (count - 1)
    flips = order_ref[0:1, 0:1] >> low & (count - 1)
    return [flips ^ step_of(mine, -hop if ring else hop, count, ring) for hop in (*sending_order(count, ring), 0)]


def merge_kernel(kappa, low, count, ring, next_ring, order_ref, *refs):
    held, out = refs[:count], refs[count:]
    places = places_of(order_ref, low, count, ring)
    fan = len(out)
    mine = lax.axis_index("depth") >> (low + count.bit_length() - 1) & (fan - 1)
    for hop in range(fan):
        for row in range(out[hop].shape[1]):
            at = row * fan + step_of(mine, hop, fan, next_ring)
            merged = over(kappa, places, [[piece[channel, at] for channel in range(3)] for piece in held])
            for channel in range(3):
                out[hop][channel, row] = merged[channel]


def opacity(depth):
    series = 1.0 - depth * (1.0 / 6.0)
    for term in (5.0, 4.0, 3.0, 2.0):
        series = 1.0 - depth * (1.0 / term) * series
    return jnp.where(depth < 0.125, depth * series, 1.0 - jnp.exp(-depth))


def glow_kernel(share_rows, offset_ref, ambient_ref, diffuse_ref, glow_ref):
    shape = glow_ref.shape[2:]
    row = lax.broadcasted_iota(jnp.int32, shape, 0) % share_rows + lax.axis_index("depth") * share_rows
    row = (row + offset_ref[0:1, 0:1]).astype(jnp.float32)
    source = 0.6 + 0.4 * jnp.cos(2.0 * math.pi * row / 64.0)
    for channel in range(3):
        glow_ref[0, channel] = jnp.broadcast_to(ambient_ref[0:1, channel : channel + 1], shape)
        glow_ref[1, channel] = diffuse_ref[0:1, channel : channel + 1] * source


def finish_kernel(kappa, low, count, ring, order_ref, glow_ref, *refs):
    held, image = refs[:count], refs[count]
    places = places_of(order_ref, low, count, ring)
    base, lit, column = over(kappa, places, [[piece[channel, 0] for channel in range(3)] for piece in held])
    share_rows = image.shape[1]
    for channel in range(4):
        if channel < 3:
            value = glow_ref[0, channel] * base + glow_ref[1, channel] * lit
        else:
            value = opacity(kappa * column)
        for j in range(image.shape[2] // LANES):
            image[channel, :, j * LANES : (j + 1) * LANES] = value[j * share_rows : (j + 1) * share_rows]


def on_device(density, clip_flags, band_offset, order, ambient, diffuse):
    slices, rows, cells = density.shape
    depth_n = lax.axis_size("depth")
    xs_n = lax.axis_size("xs")
    kappa = 2.0 / (slices * depth_n)
    extinct = 2.0 / (cells * xs_n)
    share_rows = rows // depth_n
    levels = depth_n.bit_length() - 1
    my_slab = lax.axis_index("depth")
    nearer = None
    if xs_n > 1:
        blocks_r, blocks_x = clip_flags.shape[1:]
        kept = density.astype(jnp.float32).reshape(
            slices, blocks_r, rows // blocks_r, blocks_x, cells // blocks_x
        )
        totals = jnp.sum(kept, axis=4) * clip_flags[:, :, None, :].astype(jnp.float32)
        totals = jnp.sum(totals, axis=3).reshape(slices, rows)
        nearer = prefix(totals, "xs", lambda early, late: early + late, jnp.zeros_like(totals))
        nearer = nearer[:, :, None]
    held = sent_and_held(composite_slab(clip_flags, density, nearer, kappa, extinct, depth_n), 0, False)
    first = order[None]
    vmem = pl.BlockSpec(memory_space=pltpu.VMEM)
    low, ring = 0, False
    while True:
        count = len(held)
        through = low + count.bit_length() - 1
        if through == levels:
            break
        fan = 4 if through + 1 < levels else 2
        next_ring = low > 0 and fan == 4
        shape = (3, held[0].shape[1] // fan, *held[0].shape[2:])
        pieces = pl.pallas_call(
            functools.partial(merge_kernel, kappa, low, count, ring, next_ring),
            out_shape=[pltpu.VMEM(shape, jnp.float32)] * fan,
            in_specs=[vmem] * (1 + count),
            out_specs=[vmem] * fan,
            compiler_params=pltpu.CompilerParams(vmem_limit_bytes=4 * 2**20),
            name="merge",
        )(first, *held)
        low, ring = through, next_ring
        held = sent_and_held(pieces, low, ring)
    glow = pl.pallas_call(
        functools.partial(glow_kernel, share_rows),
        out_shape=pltpu.VMEM((2, 3, share_rows * cells // LANES, LANES), jnp.float32),
        in_specs=[vmem] * 3,
        out_specs=vmem,
        compiler_params=pltpu.CompilerParams(vmem_limit_bytes=4 * 2**20),
        cost_estimate=pl.CostEstimate(flops=10**5, bytes_accessed=10**5, transcendentals=2048),
        name="glow",
    )(band_offset[None], ambient[None], diffuse[None])
    return pl.pallas_call(
        functools.partial(finish_kernel, kappa, low, len(held), ring),
        out_shape=jax.ShapeDtypeStruct((4, share_rows, cells), jnp.float32),
        in_specs=[vmem] * (2 + len(held)),
        compiler_params=pltpu.CompilerParams(vmem_limit_bytes=4 * 2**20),
        name="finish",
    )(first, glow, *held)


def solution(mesh):
    return jax.shard_map(
        on_device,
        mesh=mesh,
        in_specs=(P("depth", None, "xs"), P("depth", None, "xs"), P(), P(), P(), P()),
        out_specs=P(None, "depth", "xs"),
        check_vma=False,
    )
```

```python
import functools
import math

import jax
import jax.numpy as jnp
from jax import lax
from jax.experimental import pallas as pl
from jax.experimental.pallas import tpu as pltpu

from jax.sharding import PartitionSpec as P

LANES = 128

def prefix(value, axis, join, neutral):
    count, mine = (lax.axis_size(axis), lax.axis_index(axis))
    pieces = lax.all_gather(value, axis)
    so_far = jnp.full_like(value, 0) + jnp.asarray(neutral, value.dtype)

    def lap(position, so_far):
        longer = join(so_far, pieces[position])
        return jnp.where(position < mine, longer, so_far)

    return lax.fori_loop(0, count - 1, lap, so_far)


def slab_kernel(depth_scale, light_scale, share_rows, has_nearer, flags_hbm, dens_ref, *rest):
    if has_nearer:
        nearer_ref, *rest = rest
    keep_ref, give_ref, dens, masked, inside, upper, flags, sems, flag_sem = rest
    slices, rows, cells = dens.shape
    blocks_r, blocks_x = flags.shape[:2]
    band = rows // blocks_r
    width = cells // blocks_x
    span = math.gcd(cells, 2 * LANES)
    group = masked.shape[1] // band
    tall = group * band
    shares = band // share_rows

    def copy(part):
        at = pl.ds(0, tall) if part == 0 else pl.ds(tall, rows - tall)
        return pltpu.make_async_copy(dens_ref.at[:, at, :], dens.at[:, at, :], sems.at[part])

    flag_copy = pltpu.make_async_copy(flags_hbm, flags, flag_sem)
    flag_copy.start()
    copy(0).start()
    copy(1).start()
    upper[...] = (
        lax.broadcasted_iota(jnp.int32, (cells, cells), 0) < lax.broadcasted_iota(jnp.int32, (cells, cells), 1)
    ).astype(jnp.float32).astype(jnp.bfloat16)
    odd = lax.axis_index("depth") & 1 == 1
    flag_copy.wait()

    def work(step, carry):
        @pl.when(step == 0)
        def _():
            copy(0).wait()

        @pl.when(step == 1)
        def _():
            copy(1).wait()

        for g in range(group):
            block = step * group + g
            at = pl.ds(pl.multiple_of(block * band, band), band)
            for j in range(blocks_x):
                for z in range(slices):
                    flag = flags[block, j, z].astype(jnp.float32)
                    flag = jnp.full((band, width), flag, jnp.float32).astype(jnp.bfloat16)
                    cols = slice(j * width, (j + 1) * width)
                    masked[z, g * band : (g + 1) * band, cols] = dens[z, at, cols] * flag
        for h in range(cells // span):
            lhs = masked[:, :, : (h + 1) * span].reshape(slices * tall, (h + 1) * span)
            cols = slice(h * span, (h + 1) * span)
            inside[:, :, cols] = jnp.dot(
                lhs, upper[: (h + 1) * span, cols], preferred_element_type=jnp.float32
            ).reshape(slices, tall, span)
        for g in range(group):
            sub = slice(g * band, (g + 1) * band)
            at = pl.ds(pl.multiple_of((step * group + g) * band, band), band)
            outs = []
            for j in range(cells // LANES):
                cols = slice(j * LANES, (j + 1) * LANES)
                before = jnp.zeros((band, LANES), jnp.float32)
                through = jnp.ones((band, LANES), jnp.float32)
                base = jnp.zeros((band, LANES), jnp.float32)
                lit = jnp.zeros((band, LANES), jnp.float32)
                for z in range(slices):
                    clipped = masked[z, sub, cols].astype(jnp.float32)
                    before = before + clipped
                    behind = jnp.exp2(before * depth_scale)
                    emitted = clipped * (through - behind)
                    through = behind
                    shade = inside[z, sub, cols]
                    if has_nearer:
                        shade = shade + nearer_ref[z, at, :]
                    base = base + emitted
                    lit = lit + emitted * jnp.exp2(shade * light_scale)
                outs.append((base, lit, before))
            for channel in range(3):
                for pair in range(shares // 2):
                    halves = []
                    for side in range(2):
                        first = (2 * pair + side) * share_rows
                        halves.append(jnp.concatenate([o[channel][first : first + share_rows] for o in outs], axis=0))
                    to = (step * group + g) * (shares // 2) + pair
                    keep_ref[channel, to] = jnp.where(odd, halves[1], halves[0])
                    give_ref[channel, to] = jnp.where(odd, halves[0], halves[1])
        return carry

    lax.fori_loop(0, rows // tall, work, 0)


def composite_slab(clip_flags, density, nearer, kappa, extinct, depth_n):
    slices, rows, cells = density.shape
    share_rows = rows // depth_n
    blocks_r, blocks_x = clip_flags.shape[1:]
    half = (3, depth_n // 2, share_rows * cells // LANES, LANES)
    log2e = math.log2(math.e)
    has_nearer = nearer is not None
    tall = math.gcd(blocks_r, 2) * rows // blocks_r
    vmem = pl.BlockSpec(memory_space=pltpu.VMEM)
    return pl.pallas_call(
        functools.partial(slab_kernel, -kappa * log2e, -extinct * log2e, share_rows, has_nearer),
        out_shape=[pltpu.VMEM(half, jnp.float32)] * 2,
        in_specs=[pl.BlockSpec(memory_space=pltpu.HBM)] * 2 + [vmem] * has_nearer,
        out_specs=[vmem, vmem],
        scratch_shapes=[
            pltpu.VMEM((slices, rows, cells), jnp.bfloat16),
            pltpu.VMEM((slices, tall, cells), jnp.bfloat16),
            pltpu.VMEM((slices, tall, cells), jnp.float32),
            pltpu.VMEM((cells, cells), jnp.bfloat16),
            pltpu.SMEM((blocks_r, blocks_x, slices), jnp.int32),
            pltpu.SemaphoreType.DMA((2,)),
            pltpu.SemaphoreType.DMA,
        ],
        compiler_params=pltpu.CompilerParams(vmem_limit_bytes=24 * 2**20),
        cost_estimate=pl.CostEstimate(
            flops=2 * slices * rows * cells * cells,
            bytes_accessed=2 * slices * rows * cells,
            transcendentals=2 * slices * rows * cells,
        ),
        name="slab",
    )(
        pltpu.with_memory_space_constraint(clip_flags.transpose(1, 2, 0), pltpu.HBM),
        pltpu.with_memory_space_constraint(density, pltpu.HBM),
        *([nearer] if has_nearer else []),
    )


def step_of(position, hop, count, ring, odd):
    if ring:
        turn = ((position & 1) << 1 | position >> 1) + hop & 3
        return (turn & 1) << 1 | turn >> 1
    if count == 4 and hop in (1, 2):
        return position ^ hop ^ 3 * odd
    return position ^ hop


def sending_order(count, ring):
    if count < 4:
        return (1,)
    return (1, 3, 2) if ring else (3, 2, 1)


def sent_and_held(pieces, low, ring):
    depth_n = lax.axis_size("depth")
    count = len(pieces)
    held = []
    for hop in sending_order(count, ring):
        pairs = []
        for source in range(depth_n):
            position = source >> low & (count - 1)
            pairs.append((source, source + ((step_of(position, hop, count, ring, source & 1) - position) << low)))
        held.append(lax.ppermute(pieces[hop], "depth", pairs))
    return [*held, pieces[0]]


def over(kappa, places, held):
    base, lit, column = 0.0, 0.0, 0.0
    for place, piece in zip(places, held):
        ahead = 0.0
        for other, front in zip(places, held):
            if front is not piece:
                ahead = ahead + jnp.where(other < place, front[2], 0.0)
        passed = jnp.exp(-kappa * ahead)
        base = base + piece[0] * passed
        lit = lit + piece[1] * passed
        column = column + piece[2]
    return base, lit, column


def places_of(order_ref, low, count, ring):
    mine = lax.axis_index("depth") >> low & (count - 1)
    flips = order_ref[0:1, 0:1] >> low & (count - 1)
    odd = lax.axis_index("depth") & 1
    return [flips ^ step_of(mine, -hop if ring else hop, count, ring, odd) for hop in (*sending_order(count, ring), 0)]


def merge_kernel(kappa, low, count, ring, next_ring, order_ref, *refs):
    held, out = refs[:count], refs[count:]
    places = places_of(order_ref, low, count, ring)
    fan = len(out)
    mine = lax.axis_index("depth") >> (low + count.bit_length() - 1) & (fan - 1)
    for hop in range(fan):
        for row in range(out[hop].shape[1]):
            at = row * fan + step_of(mine, hop, fan, next_ring, lax.axis_index("depth") & 1)
            merged = over(kappa, places, [[piece[channel, at] for channel in range(3)] for piece in held])
            for channel in range(3):
                out[hop][channel, row] = merged[channel]


def opacity(depth):
    series = 1.0 - depth * (1.0 / 6.0)
    for term in (5.0, 4.0, 3.0, 2.0):
        series = 1.0 - depth * (1.0 / term) * series
    return jnp.where(depth < 0.125, depth * series, 1.0 - jnp.exp(-depth))


def glow_kernel(share_rows, offset_ref, ambient_ref, diffuse_ref, glow_ref):
    shape = glow_ref.shape[2:]
    row = lax.broadcasted_iota(jnp.int32, shape, 0) % share_rows + lax.axis_index("depth") * share_rows
    row = (row + offset_ref[0:1, 0:1]).astype(jnp.float32)
    source = 0.6 + 0.4 * jnp.cos(2.0 * math.pi * row / 64.0)
    for channel in range(3):
        glow_ref[0, channel] = jnp.broadcast_to(ambient_ref[0:1, channel : channel + 1], shape)
        glow_ref[1, channel] = diffuse_ref[0:1, channel : channel + 1] * source


def finish_kernel(kappa, low, count, ring, order_ref, glow_ref, *refs):
    held, image = refs[:count], refs[count]
    places = places_of(order_ref, low, count, ring)
    base, lit, column = over(kappa, places, [[piece[channel, 0] for channel in range(3)] for piece in held])
    share_rows = image.shape[1]
    for channel in range(4):
        if channel < 3:
            value = glow_ref[0, channel] * base + glow_ref[1, channel] * lit
        else:
            value = opacity(kappa * column)
        for j in range(image.shape[2] // LANES):
            image[channel, :, j * LANES : (j + 1) * LANES] = value[j * share_rows : (j + 1) * share_rows]


def on_device(density, clip_flags, band_offset, order, ambient, diffuse):
    slices, rows, cells = density.shape
    depth_n = lax.axis_size("depth")
    xs_n = lax.axis_size("xs")
    kappa = 2.0 / (slices * depth_n)
    extinct = 2.0 / (cells * xs_n)
    share_rows = rows // depth_n
    levels = depth_n.bit_length() - 1
    my_slab = lax.axis_index("depth")
    nearer = None
    if xs_n > 1:
        blocks_r, blocks_x = clip_flags.shape[1:]
        kept = density.astype(jnp.float32).reshape(
            slices, blocks_r, rows // blocks_r, blocks_x, cells // blocks_x
        )
        totals = jnp.sum(kept, axis=4) * clip_flags[:, :, None, :].astype(jnp.float32)
        totals = jnp.sum(totals, axis=3).reshape(slices, rows)
        nearer = prefix(totals, "xs", lambda early, late: early + late, jnp.zeros_like(totals))
        nearer = nearer[:, :, None]
    held = sent_and_held(composite_slab(clip_flags, density, nearer, kappa, extinct, depth_n), 0, False)
    first = order[None]
    vmem = pl.BlockSpec(memory_space=pltpu.VMEM)
    low, ring = 0, False
    while True:
        count = len(held)
        through = low + count.bit_length() - 1
        if through == levels:
            break
        fan = 4 if through + 1 < levels else 2
        next_ring = low > 0 and fan == 4
        shape = (3, held[0].shape[1] // fan, *held[0].shape[2:])
        pieces = pl.pallas_call(
            functools.partial(merge_kernel, kappa, low, count, ring, next_ring),
            out_shape=[pltpu.VMEM(shape, jnp.float32)] * fan,
            in_specs=[vmem] * (1 + count),
            out_specs=[vmem] * fan,
            compiler_params=pltpu.CompilerParams(vmem_limit_bytes=4 * 2**20),
            name="merge",
        )(first, *held)
        low, ring = through, next_ring
        held = sent_and_held(pieces, low, ring)
    glow = pl.pallas_call(
        functools.partial(glow_kernel, share_rows),
        out_shape=pltpu.VMEM((2, 3, share_rows * cells // LANES, LANES), jnp.float32),
        in_specs=[vmem] * 3,
        out_specs=vmem,
        compiler_params=pltpu.CompilerParams(vmem_limit_bytes=4 * 2**20),
        cost_estimate=pl.CostEstimate(flops=10**5, bytes_accessed=10**5, transcendentals=2048),
        name="glow",
    )(band_offset[None], ambient[None], diffuse[None])
    return pl.pallas_call(
        functools.partial(finish_kernel, kappa, low, len(held), ring),
        out_shape=jax.ShapeDtypeStruct((4, share_rows, cells), jnp.float32),
        in_specs=[vmem] * (2 + len(held)),
        compiler_params=pltpu.CompilerParams(vmem_limit_bytes=4 * 2**20),
        name="finish",
    )(first, glow, *held)


def solution(mesh):
    return jax.shard_map(
        on_device,
        mesh=mesh,
        in_specs=(P("depth", None, "xs"), P("depth", None, "xs"), P(), P(), P(), P()),
        out_specs=P(None, "depth", "xs"),
        check_vma=False,
    )
```
